256 devices in a mesh: gx: 16 (over y_hi, x, core), yz: 16 (over z, y_lo).
Axes of the slice: x: 4, y: 4 (y_hi: 2, y_lo: 2; y = y_hi * 2 + y_lo), z: 8, core: 2. Of those that a mesh axis runs over, the one named last changes fastest.
Arguments:
- vectors: float32 [8, 256, 256, 512], P(None, 'gx', 'yz'), may hold values from -4 to 4
- classes: int32 [256, 256, 512], P('gx', 'yz'), may hold values from 0 to 3
- permittivity: float32 [4], replicated, may hold values from 0.01 to 10
Outputs:
- applied: float32 [8, 256, 256, 512], P(None, 'gx', 'yz')
- coarse: float32 [2048, 2048], P('gx', 'yz')
The draws below stay inside these ranges and needn't reach their ends.
All inputs are finite; a program needn't handle non-finite values.
Results may differ from the reference program's by a relative error of at most 0.000071.
Values sent between devices are 32-bit elements; how exact they have to be, the bound alone decides.
No kernel may reach another device: no remote copies, remote signals or barrier semaphores. Data moves between devices by JAX's collectives and lax.ppermute only.
A program may use at most 64 MiB of HBM per device.

```python
import math
import jax
import jax.numpy as jnp
from jax import lax

K = 8
NCLASS = 4
CX = 16
CZ = 16
NY = 512
NX = 256
NZ = 256


def draw_vectors(key, part):
    key = jax.random.fold_in(key, 11)
    first_key, second_key = jax.random.split(key, 2)
    segment = NY // 8
    level_shape = (K, NX // CX, NZ // CZ, 8)
    level = jax.random.uniform(first_key, level_shape, jnp.float32, -2.0, 2.0)
    noise = 0.5 * jax.random.truncated_normal(second_key, -3.0, 3.0, (K, NX, NZ, NY), jnp.float32)
    level = jnp.repeat(jnp.repeat(jnp.repeat(level, CX, axis=1), CZ, axis=2), segment, axis=3)
    return (level + noise).astype(jnp.float32)


def place_ends(drawn, key, low, largest):
    shape = drawn.shape
    index_at = [jax.random.randint(jax.random.fold_in(key, axis), (), 0, shape[axis]) for axis in range(len(shape))]
    drawn = drawn.at[tuple(index_at)].set(low)
    longest = shape.index(max(shape))
    index_at[longest] = (index_at[longest] + 1) % shape[longest]
    return drawn.at[tuple(index_at)].set(largest)


def setup_inputs(seed: int = 0) -> dict:
    keys = jax.random.split(jax.random.key(seed), 4)
    vectors = draw_vectors(jax.random.fold_in(keys[3], 71), 0)
    classes = place_ends(jax.random.randint(keys[1], (NX, NZ, NY), 0, NCLASS), jax.random.fold_in(keys[1], 1), 0, NCLASS - 1).astype(jnp.int32)
    permittivity = jnp.clip(jnp.exp(jax.random.uniform(keys[2], (NCLASS,), jnp.float32, math.log(0.01), math.log(10.0))), 0.01, 10.0)
    return {"vectors": vectors, "classes": classes, "permittivity": permittivity}


def permit(classes, permittivity):
    onehot = (classes[..., None] == jnp.arange(permittivity.shape[0], dtype=jnp.int32)).astype(jnp.float32)
    return jnp.sum(onehot * permittivity, axis=-1)


def harmonic(first_value, second_value):
    return 2.0 * first_value * second_value / (first_value + second_value)


def reference(vectors, classes, permittivity):
    highest = lax.Precision.HIGHEST
    vector_count = vectors.shape[0]
    x_blocks = NX // CX
    z_blocks = NZ // CZ
    epsilon = permit(classes, permittivity)
    face_x = harmonic(epsilon[:-1], epsilon[1:])
    face_z = harmonic(epsilon[:, :-1], epsilon[:, 1:])
    face_y = harmonic(epsilon[:, :, :-1], epsilon[:, :, 1:])
    keep_x = ((jnp.arange(NX - 1) + 1) % CX != 0).astype(jnp.float32)[:, None, None]
    keep_z = ((jnp.arange(NZ - 1) + 1) % CZ != 0).astype(jnp.float32)[None, :, None]
    applied = jnp.zeros_like(vectors)
    applied = applied.at[:, :-1].add(face_x * (vectors[:, :-1] - keep_x * vectors[:, 1:]))
    applied = applied.at[:, 1:].add(face_x * (vectors[:, 1:] - keep_x * vectors[:, :-1]))
    applied = applied.at[:, :, :-1].add(face_z * (vectors[:, :, :-1] - keep_z * vectors[:, :, 1:]))
    applied = applied.at[:, :, 1:].add(face_z * (vectors[:, :, 1:] - keep_z * vectors[:, :, :-1]))
    applied = applied.at[:, :, :, :-1].add(face_y * (vectors[:, :, :, :-1] - vectors[:, :, :, 1:]))
    applied = applied.at[:, :, :, 1:].add(face_y * (vectors[:, :, :, 1:] - vectors[:, :, :, :-1]))
    shaped = (vector_count, x_blocks, CX, z_blocks, CZ, NY)
    self_block = jnp.einsum("kaibjy,laibjy->abkl", vectors.reshape(shaped), applied.reshape(shaped), precision=highest)
    left_face = vectors[:, CX - 1:NX - 1:CX] * face_x[CX - 1::CX]
    right_face = vectors[:, CX:NX:CX]
    xshape = (vector_count, x_blocks - 1, z_blocks, CZ, NY)
    upper_x = -jnp.einsum("kabjy,labjy->abkl", left_face.reshape(xshape), right_face.reshape(xshape), precision=highest)
    low_face = vectors[:, :, CZ - 1:NZ - 1:CZ] * face_z[:, CZ - 1::CZ]
    high_face = vectors[:, :, CZ:NZ:CZ]
    zshape = (vector_count, x_blocks, CX, z_blocks - 1, NY)
    upper_z = -jnp.einsum("kaiby,laiby->abkl", low_face.reshape(zshape), high_face.reshape(zshape), precision=highest)
    coarse_full = jnp.zeros((x_blocks, z_blocks, vector_count, x_blocks, z_blocks, vector_count), jnp.float32)
    index_a, index_b = jnp.meshgrid(jnp.arange(x_blocks), jnp.arange(z_blocks), indexing="ij")
    coarse_full = coarse_full.at[index_a, index_b, :, index_a, index_b, :].set(self_block)
    index_a, index_b = jnp.meshgrid(jnp.arange(x_blocks - 1), jnp.arange(z_blocks), indexing="ij")
    coarse_full = coarse_full.at[index_a, index_b, :, index_a + 1, index_b, :].set(upper_x)
    coarse_full = coarse_full.at[index_a + 1, index_b, :, index_a, index_b, :].set(jnp.swapaxes(upper_x, -1, -2))
    index_a, index_b = jnp.meshgrid(jnp.arange(x_blocks), jnp.arange(z_blocks - 1), indexing="ij")
    coarse_full = coarse_full.at[index_a, index_b, :, index_a, index_b + 1, :].set(upper_z)
    coarse_full = coarse_full.at[index_a, index_b + 1, :, index_a, index_b, :].set(jnp.swapaxes(upper_z, -1, -2))
    order_total = vector_count * x_blocks * z_blocks
    coarse = coarse_full.reshape(order_total, order_total) / (CZ * NY)
    return applied, coarse
```

```python
import functools
import jax
import jax.numpy as jnp
from jax import lax
from jax.experimental import pallas as pl
from jax.experimental.pallas import tpu as pltpu
from jax.sharding import PartitionSpec as P

F32 = jnp.float32
BF16 = jnp.bfloat16


def harmonic(first_value, second_value):
    return 2.0 * first_value * second_value / (first_value + second_value)


def permit(classes, table):
    value = jnp.where(classes == 0, table[0], 0.0)
    for index in range(1, table.shape[0]):
        value = jnp.where(classes == index, table[index], value)
    return value


def split(rows):
    high = rows.astype(BF16)
    low = (rows - high.astype(F32)).astype(BF16)
    return jnp.concatenate([high, low], axis=0)


def products(left, right):
    return lax.dot_general(left, right, (((1,), (1,)), ((), ())), preferred_element_type=F32)


def fold(full, count, points):
    size = count * points
    total = (full[:size, :size] + full[:size, size:]) + (full[size:, :size] + full[size:, size:])
    row = lax.broadcasted_iota(jnp.int32, (size, size), 0)
    column = lax.broadcasted_iota(jnp.int32, (size, size), 1)
    total = jnp.where(lax.rem(row, points) == lax.rem(column, points), total, 0.0)
    return jnp.sum(total.reshape(count, points, size), axis=1)


def faces_kernel(table, vectors, classes, x_high, x_low, z_high, z_low, held, values, sems):
    count, cells_x, cells_z, _ = vectors.shape
    copies = [
        pltpu.make_async_copy(vectors.at[:, :, cells_z - 1], z_high.at[0:count], sems.at[0]),
        pltpu.make_async_copy(vectors.at[:, cells_x - 1], x_high.at[0:count], sems.at[1]),
        pltpu.make_async_copy(vectors.at[:, 0], x_low.at[0:count], sems.at[2]),
    ]
    layers = [
        pltpu.make_async_copy(classes.at[:, cells_z - 1], held.at[0], sems.at[3]),
        pltpu.make_async_copy(classes.at[cells_x - 1], held.at[1], sems.at[4]),
        pltpu.make_async_copy(classes.at[0], held.at[2], sems.at[5]),
        pltpu.make_async_copy(classes.at[:, 0], held.at[3], sems.at[6]),
    ]
    for copy in layers + copies:
        copy.start()
    places = [z_high.at[count], x_high.at[count], x_low.at[count], z_low]
    for index, (layer, place) in enumerate(zip(layers, places)):
        layer.wait()
        values[index] = permit(held[index], table)
        copy = pltpu.make_async_copy(values.at[index], place, sems.at[7 + index])
        copy.start()
        copies.append(copy)
    for copy in copies:
        copy.wait()


def block_kernel(
    chunks, table, vectors, classes, applied, own, z_face, x_sums, z_sums, held, kinds, face_x, result, total, sems
):
    count, cells_x, cells_z, length = vectors.shape
    step = cells_x // chunks
    kind_copy = pltpu.make_async_copy(classes, kinds, sems.at[0])
    kind_copy.start()
    loads, stores = [], []
    for chunk in range(chunks):
        planes = pl.ds(chunk * step, step)
        load = pltpu.make_async_copy(vectors.at[:, planes], held.at[:, planes], sems.at[3 + chunk])
        load.start()
        loads.append(load)
        stores.append(
            pltpu.make_async_copy(result.at[:, planes], applied.at[:, planes], sems.at[3 + chunks + chunk])
        )
    face_copy = pltpu.make_async_copy(vectors.at[:, :, 0], z_face, sems.at[1])
    face_copy.start()
    face_x[0] = jnp.zeros((cells_z, length), F32)
    total[...] = jnp.zeros_like(total)
    row = lax.broadcasted_iota(jnp.int32, (cells_z, length), 0)
    column = lax.broadcasted_iota(jnp.int32, (cells_z, length), 1)
    kind_copy.wait()

    def plane(index, carry):
        before = jnp.maximum(index - 1, 0)
        after = jnp.minimum(index + 1, cells_x - 1)
        value = permit(kinds[index], table)
        value_after = permit(kinds[after], table)
        low_x = face_x[index]
        high_x = jnp.where(index + 1 < cells_x, harmonic(value, value_after), 0.0)
        face_x[index + 1] = high_x
        value_z = pltpu.roll(value, cells_z - 1, 0)
        value_y = pltpu.roll(value, length - 1, 1)
        high_z = jnp.where(row < cells_z - 1, harmonic(value, value_z), 0.0)
        high_y = jnp.where(column < length - 1, harmonic(value, value_y), 0.0)
        for k in range(count):
            here = held[k, index]
            flux = low_x * (here - held[k, before]) + high_x * (here - held[k, after])
            flux_z = high_z * (here - pltpu.roll(here, cells_z - 1, 0))
            flux = flux + (flux_z - pltpu.roll(flux_z, 1, 0))
            flux_y = high_y * (here - pltpu.roll(here, length - 1, 1))
            flux = flux + (flux_y - pltpu.roll(flux_y, 1, 1))
            result[k, index] = flux
        left = split(held[:, index].reshape(count * cells_z, length))
        right = split(result[:, index].reshape(count * cells_z, length))
        total[...] += products(left, right)
        return carry

    loads[0].wait()
    for chunk in range(chunks):
        if chunk + 1 < chunks:
            loads[chunk + 1].wait()
        lax.fori_loop(chunk * step, (chunk + 1) * step, plane, 0)
        stores[chunk].start()
    sides = [
        pltpu.make_async_copy(result.at[:, 0], x_sums.at[0], sems.at[3 + 2 * chunks]),
        pltpu.make_async_copy(result.at[:, cells_x - 1], x_sums.at[1], sems.at[4 + 2 * chunks]),
        pltpu.make_async_copy(result.at[:, :, 0], z_sums.at[0], sems.at[5 + 2 * chunks]),
        pltpu.make_async_copy(result.at[:, :, cells_z - 1], z_sums.at[1], sems.at[6 + 2 * chunks]),
    ]
    for copy in sides:
        copy.start()
    own[...] = fold(total[...], count, cells_z)
    for copy in [face_copy] + sides + stores:
        copy.wait()


def outer_kernel(
    place, applied_in, own, z_face, x_sums, z_sums, x_high, x_low, z_high, z_low,
    from_x_low, from_x_high, from_z_low, from_z_high, applied, blocks, x_new, z_new, sems,
):
    count, cells_x, cells_z, length = applied.shape
    slots, _, width = blocks.shape
    slab, tile = place[0], place[1]
    last_slab, last_tile = place[2], place[3]
    low_x = jnp.where(slab > 0, harmonic(x_low[count], from_x_low[count]), 0.0)
    high_x = jnp.where(slab < last_slab, harmonic(x_high[count], from_x_high[count]), 0.0)
    low_z = jnp.where(tile > 0, harmonic(z_low[...], from_z_low[count]), 0.0)
    high_z = jnp.where(tile < last_tile, harmonic(z_high[count], from_z_high[...]), 0.0)
    flux_near = z_face[...] * low_z
    flux_far = z_high[0:count] * high_z
    z_new[0] = z_sums[0] + flux_near
    z_new[1] = z_sums[1] + flux_far
    z_stores = [
        pltpu.make_async_copy(z_new.at[0], applied.at[:, :, 0], sems.at[0]),
        pltpu.make_async_copy(z_new.at[1], applied.at[:, :, cells_z - 1], sems.at[1]),
    ]
    for copy in z_stores:
        copy.start()
    flux_low = x_low[0:count] * low_x
    flux_high = x_high[0:count] * high_x
    x_new[0] = x_sums[0] + flux_low
    x_new[1] = x_sums[1] + flux_high
    for side, at in ((0, 0), (1, cells_x - 1)):
        x_new[side, :, 0:1, :] += flux_near[:, at : at + 1, :]
        x_new[side, :, cells_z - 1 : cells_z, :] += flux_far[:, at : at + 1, :]

    def rows(block):
        return block.reshape(count * block.shape[1], length)

    left_near, left_far = split(rows(flux_near)), split(rows(flux_far))
    own_z = products(left_near, split(rows(z_face[...]))) + products(left_far, split(rows(z_high[0:count])))
    cross_z = fold(products(left_near, split(rows(from_z_low[0:count]))), count, cells_x)
    for copy in z_stores:
        copy.wait()
    x_stores = [
        pltpu.make_async_copy(x_new.at[0], applied.at[:, 0], sems.at[2]),
        pltpu.make_async_copy(x_new.at[1], applied.at[:, cells_x - 1], sems.at[3]),
    ]
    for copy in x_stores:
        copy.start()
    left_low, left_high = split(rows(flux_low)), split(rows(flux_high))
    own_x = products(left_low, split(rows(x_low[0:count]))) + products(left_high, split(rows(x_high[0:count])))
    cross_low = fold(products(left_low, split(rows(from_x_low[0:count]))), count, cells_z)
    cross_high = fold(products(left_high, split(rows(from_x_high[0:count]))), count, cells_z)
    self_rows = own[...] + fold(own_x, count, cells_z)
    self_z = fold(own_z, count, cells_x)

    scale = 1.0 / (cells_z * length)
    entry = lax.broadcasted_iota(jnp.int32, (count * cells_z, width), 0)
    column = lax.broadcasted_iota(jnp.int32, (count * cells_z, width), 1)
    here = (lax.div(entry, cells_z) + tile * count == column).astype(F32)
    entry = lax.broadcasted_iota(jnp.int32, (count * cells_x, width), 0)
    column = lax.broadcasted_iota(jnp.int32, (count * cells_x, width), 1)
    here_z = (lax.div(entry, cells_x) + tile * count == column).astype(F32)
    before_z = (lax.div(entry, cells_x) + (tile - 1) * count == column).astype(F32)
    highest = lax.Precision.HIGHEST
    stacked = jnp.concatenate([self_rows, -cross_low, -cross_high], axis=0)
    placed = jnp.dot(stacked, here, precision=highest, preferred_element_type=F32) * scale
    placed_z = jnp.dot(
        jnp.concatenate([self_z, -cross_z], axis=1),
        jnp.concatenate([here_z, before_z], axis=0),
        precision=highest,
        preferred_element_type=F32,
    )
    blocks[...] = jnp.zeros_like(blocks)
    blocks[slab] = placed[0:count] + placed_z * scale

    @pl.when(slab > 0)
    def _():
        blocks[slab - 1] = placed[count : 2 * count]

    @pl.when(slab < last_slab)
    def _():
        blocks[slab + 1] = placed[2 * count : 3 * count]

    for copy in x_stores:
        copy.wait()


def finish_kernel(count, tile, coarse):
    size = tile.shape[0]
    row = lax.broadcasted_iota(jnp.int32, (size, size), 0)
    column = lax.broadcasted_iota(jnp.int32, (size, size), 1)
    value = tile[...]
    other = jnp.where(lax.div(row, count) == lax.div(column, count), 0.0, value.T)
    coarse[...] = value + other


def shards(vectors, classes, permittivity):
    count, cells_x, cells_z, length = vectors.shape
    slabs, tiles = lax.axis_size("gx"), lax.axis_size("yz")
    hbm = pl.BlockSpec(memory_space=pltpu.HBM)
    anywhere = pl.BlockSpec(memory_space=pl.ANY)
    smem = pl.BlockSpec(memory_space=pltpu.SMEM)
    vmem = pl.BlockSpec(memory_space=pltpu.VMEM)
    shape = jax.ShapeDtypeStruct
    limit = 24 * 1024 * 1024
    params = pltpu.CompilerParams(vmem_limit_bytes=limit)
    vectors = pltpu.with_memory_space_constraint(vectors, pltpu.HBM)
    classes = pltpu.with_memory_space_constraint(classes, pltpu.HBM)

    x_high, x_low, z_high, z_low = pl.pallas_call(
        faces_kernel,
        out_shape=(
            shape((count + 1, cells_z, length), F32),
            shape((count + 1, cells_z, length), F32),
            shape((count + 1, cells_x, length), F32),
            shape((cells_x, length), F32),
        ),
        in_specs=[smem, hbm, hbm],
        out_specs=(anywhere,) * 4,
        scratch_shapes=[
            pltpu.VMEM((4, cells_z, length), jnp.int32),
            pltpu.VMEM((4, cells_z, length), F32),
            pltpu.SemaphoreType.DMA((11,)),
        ],
        compiler_params=params,
        name="faces",
    )(permittivity, vectors, classes)

    up_x = [(i, (i + 1) % slabs) for i in range(slabs)]
    up_z = [(i, (i + 1) % tiles) for i in range(tiles)]
    down_x = [(target, source) for source, target in up_x]
    down_z = [(target, source) for source, target in up_z]
    from_z_low = lax.ppermute(z_high, "yz", up_z)
    from_x_low = lax.ppermute(x_high, "gx", up_x)
    from_x_high = lax.ppermute(x_low, "gx", down_x)
    from_z_high = lax.ppermute(z_low, "yz", down_z)

    chunks = 4
    applied, own, z_face, x_sums, z_sums = pl.pallas_call(
        functools.partial(block_kernel, chunks),
        out_shape=(
            pltpu.HBM(vectors.shape, F32),
            shape((count, count * cells_z), F32),
            shape((count, cells_x, length), F32),
            shape((2, count, cells_z, length), F32),
            shape((2, count, cells_x, length), F32),
        ),
        in_specs=[smem, hbm, hbm],
        out_specs=(hbm, vmem, anywhere, anywhere, anywhere),
        scratch_shapes=[
            pltpu.VMEM(vectors.shape, F32),
            pltpu.VMEM(classes.shape, jnp.int32),
            pltpu.VMEM((cells_x + 1, cells_z, length), F32),
            pltpu.VMEM(vectors.shape, F32),
            pltpu.VMEM((2 * count * cells_z, 2 * count * cells_z), F32),
            pltpu.SemaphoreType.DMA((7 + 2 * chunks,)),
        ],
        compiler_params=params,
        cost_estimate=pl.CostEstimate(flops=5_000_000_000, bytes_accessed=20_000_000, transcendentals=0),
        name="block",
    )(permittivity, vectors, classes)

    place = jnp.stack(
        [lax.axis_index("gx"), lax.axis_index("yz"), jnp.int32(slabs - 1), jnp.int32(tiles - 1)]
    ).astype(jnp.int32)
    applied, blocks = pl.pallas_call(
        outer_kernel,
        out_shape=(pltpu.HBM(vectors.shape, F32), shape((tiles, count, count * slabs), F32)),
        in_specs=[smem, hbm] + [vmem] * 12,
        out_specs=(hbm, vmem),
        scratch_shapes=[
            pltpu.VMEM((2, count, cells_z, length), F32),
            pltpu.VMEM((2, count, cells_x, length), F32),
            pltpu.SemaphoreType.DMA((4,)),
        ],
        input_output_aliases={1: 0},
        compiler_params=params,
        name="outer",
    )(
        place, applied, own, z_face, x_sums, z_sums, x_high, x_low, z_high, z_low,
        from_x_low, from_x_high, from_z_low, from_z_high,
    )
    tile = lax.all_to_all(blocks, "yz", split_axis=0, concat_axis=0, tiled=True)
    tile = tile.reshape(tiles * count, count * slabs)
    coarse = pl.pallas_call(
        functools.partial(finish_kernel, count),
        out_shape=shape(tile.shape, F32),
        in_specs=[vmem],
        out_specs=vmem,
        compiler_params=params,
        name="finish",
    )(tile)
    return (applied, coarse)


def solution(mesh):
    return jax.shard_map(
        shards,
        mesh=mesh,
        in_specs=(P(None, "gx", "yz", None), P("gx", "yz", None), P()),
        out_specs=(P(None, "gx", "yz", None), P("gx", "yz")),
        check_vma=False,
    )
```

```python
import functools
import jax
import jax.numpy as jnp
from jax import lax
from jax.experimental import pallas as pl
from jax.experimental.pallas import tpu as pltpu
from jax.sharding import PartitionSpec as P

F32 = jnp.float32
BF16 = jnp.bfloat16


def harmonic(first_value, second_value):
    return 2.0 * first_value * second_value / (first_value + second_value)


def permit(classes, table):
    value = jnp.where(classes == 0, table[0], 0.0)
    for index in range(1, table.shape[0]):
        value = jnp.where(classes == index, table[index], value)
    return value


def split(rows):
    high = rows.astype(BF16)
    low = (rows - high.astype(F32)).astype(BF16)
    return jnp.concatenate([high, low], axis=0)


def products(left, right):
    return lax.dot_general(left, right, (((1,), (1,)), ((), ())), preferred_element_type=F32)


def fold(full, count, points):
    size = count * points
    total = (full[:size, :size] + full[:size, size:]) + (full[size:, :size] + full[size:, size:])
    row = lax.broadcasted_iota(jnp.int32, (size, size), 0)
    column = lax.broadcasted_iota(jnp.int32, (size, size), 1)
    total = jnp.where(lax.rem(row, points) == lax.rem(column, points), total, 0.0)
    return jnp.sum(total.reshape(count, points, size), axis=1)


def faces_kernel(table_in, vectors, classes, x_a, x_b, z_a, z_b, held, table, sems):
    count, cells_x, cells_z, length = vectors.shape
    half = cells_x // 2
    slab_odd = lax.rem(lax.axis_index("gx"), 2)
    tile_odd = lax.rem(lax.axis_index("yz"), 2)
    table_copy = pltpu.make_async_copy(table_in, table, sems.at[0])
    table_copy.start()
    layers, copies = [], []
    for odd in range(2):
        layer = [
            pltpu.make_async_copy(classes.at[:, (cells_z - 1) * side], held.at[index], sems.at[1 + index])
            for index, side in enumerate((1 - odd, odd))
        ]
        face = [
            pltpu.make_async_copy(
                vectors.at[:, (1 - side) * half : (2 - side) * half, (cells_z - 1) * side],
                out.at[0:count],
                sems.at[5 + index],
            )
            for index, (out, side) in enumerate(((z_a, 1 - odd), (z_b, odd)))
        ]

        @pl.when(tile_odd == odd)
        def _():
            for copy in layer + face:
                copy.start()

        if odd == 0:
            layers += layer
            copies += face
    for index, (out, side) in enumerate(((x_a, 1 - slab_odd), (x_b, slab_odd))):
        at = (cells_x - 1) * side
        layer = pltpu.make_async_copy(classes.at[at], held.at[2 + index], sems.at[3 + index])
        layer.start()
        layers.append(layer)
        face = pltpu.make_async_copy(vectors.at[:, at], out.at[0:count], sems.at[7 + index])
        face.start()
        copies.append(face)
    table_copy.wait()
    for index, out in enumerate((z_a, z_b, x_a, x_b)):
        layers[index].wait()
        out[count:] = permit(held[index], table).reshape(out.shape[0] - count, out.shape[1], length)
    for copy in copies:
        copy.wait()


def block_kernel(
    chunks, table_in, vectors, classes, applied, own, z_faces, x_sums, z_sums,
    held, kinds, face_x, result, total, table, sems,
):
    count, cells_x, cells_z, length = vectors.shape
    step = cells_x // chunks
    kind_copy = pltpu.make_async_copy(classes, kinds, sems.at[0])
    kind_copy.start()
    table_copy = pltpu.make_async_copy(table_in, table, sems.at[7 + 2 * chunks])
    table_copy.start()
    loads, stores = [], []
    for chunk in range(chunks):
        planes = pl.ds(chunk * step, step)
        load = pltpu.make_async_copy(vectors.at[:, planes], held.at[:, planes], sems.at[1 + chunk])
        load.start()
        loads.append(load)
        stores.append(
            pltpu.make_async_copy(result.at[:, planes], applied.at[:, planes], sems.at[1 + chunks + chunk])
        )
    face_x[0] = jnp.zeros((cells_z, length), F32)
    total[...] = jnp.zeros_like(total)
    row = lax.broadcasted_iota(jnp.int32, (cells_z, length), 0)
    column = lax.broadcasted_iota(jnp.int32, (cells_z, length), 1)
    kind_copy.wait()
    table_copy.wait()

    def plane(index):
        before = jnp.maximum(index - 1, 0)
        after = jnp.minimum(index + 1, cells_x - 1)
        value = permit(kinds[index], table)
        value_after = permit(kinds[after], table)
        low_x = face_x[index]
        high_x = jnp.where(index + 1 < cells_x, harmonic(value, value_after), 0.0)
        face_x[index + 1] = high_x
        value_z = pltpu.roll(value, cells_z - 1, 0)
        value_y = pltpu.roll(value, length - 1, 1)
        high_z = jnp.where(row < cells_z - 1, harmonic(value, value_z), 0.0)
        high_y = jnp.where(column < length - 1, harmonic(value, value_y), 0.0)
        for k in range(count):
            here = held[k, index]
            flux = low_x * (here - held[k, before]) + high_x * (here - held[k, after])
            flux_z = high_z * (here - pltpu.roll(here, cells_z - 1, 0))
            flux = flux + (flux_z - pltpu.roll(flux_z, 1, 0))
            flux_y = high_y * (here - pltpu.roll(here, length - 1, 1))
            flux = flux + (flux_y - pltpu.roll(flux_y, 1, 1))
            result[k, index] = flux

    def gram(index):
        left = split(held[:, index].reshape(count * cells_z, length))
        right = split(result[:, index].reshape(count * cells_z, length))
        return products(left, right)

    def follow(index, carry):
        total[...] += gram(index - 1)
        plane(index)
        return carry

    loads[0].wait()
    plane(0)
    for chunk in range(chunks):
        if chunk + 1 < chunks:
            loads[chunk + 1].wait()
        lax.fori_loop(max(1, chunk * step), (chunk + 1) * step, follow, 0)
        stores[chunk].start()
    sides = [
        pltpu.make_async_copy(result.at[:, 0], x_sums.at[0], sems.at[1 + 2 * chunks]),
        pltpu.make_async_copy(result.at[:, cells_x - 1], x_sums.at[1], sems.at[2 + 2 * chunks]),
        pltpu.make_async_copy(result.at[:, :, 0], z_sums.at[0], sems.at[3 + 2 * chunks]),
        pltpu.make_async_copy(result.at[:, :, cells_z - 1], z_sums.at[1], sems.at[4 + 2 * chunks]),
        pltpu.make_async_copy(held.at[:, :, 0], z_faces.at[0], sems.at[5 + 2 * chunks]),
        pltpu.make_async_copy(held.at[:, :, cells_z - 1], z_faces.at[1], sems.at[6 + 2 * chunks]),
    ]
    for copy in sides:
        copy.start()
    own[...] = fold(total[...] + gram(cells_x - 1), count, cells_z)
    for copy in sides + stores:
        copy.wait()


def outer_kernel(
    applied_in, own, z_faces, x_sums, z_sums, x_a, x_b, z_a, z_b, from_x_a, from_x_b, from_z_a, from_z_b,
    applied, blocks, x_new, z_new, z_flux, sems,
):
    count, cells_x, cells_z, length = applied.shape
    slots, _, width = blocks.shape
    half = cells_x // 2
    slab, tile = lax.axis_index("gx"), lax.axis_index("yz")
    slabs, tiles = lax.axis_size("gx"), lax.axis_size("yz")
    slab_odd, tile_odd = lax.rem(slab, 2), lax.rem(tile, 2)

    def rows(block):
        return block.reshape(-1, length)

    crosses_z = []
    for side, mine, other in ((1 - tile_odd, z_a, from_z_a), (tile_odd, z_b, from_z_b)):
        met = jnp.logical_and(tile + 2 * side - 1 >= 0, tile + 2 * side - 1 < tiles)
        weight = jnp.where(met, harmonic(rows(mine[count:]), rows(other[count:])), 0.0)
        flux = z_faces[side] * weight
        z_new[side] = z_sums[side] + flux
        z_flux[side] = flux.reshape(count, 2, half, length)
    z_stores = [
        pltpu.make_async_copy(z_new.at[0], applied.at[:, :, 0], sems.at[0]),
        pltpu.make_async_copy(z_new.at[1], applied.at[:, :, cells_z - 1], sems.at[1]),
    ]
    for copy in z_stores:
        copy.start()
    fluxes_x = []
    for side, mine, other in ((1 - slab_odd, x_a, from_x_a), (slab_odd, x_b, from_x_b)):
        met = jnp.logical_and(slab + 2 * side - 1 >= 0, slab + 2 * side - 1 < slabs)
        weight = jnp.where(met, harmonic(mine[count], other[count]), 0.0)
        flux = mine[0:count] * weight
        x_new[side] = x_sums[side] + flux
        fluxes_x.append(flux)
    for side, end in ((0, 0), (1, cells_x - 1)):
        part, at = divmod(end, half)
        x_new[side, :, 0:1, :] += z_flux[0, :, part, at : at + 1, :]
        x_new[side, :, cells_z - 1 : cells_z, :] += z_flux[1, :, part, at : at + 1, :]

    own_z = products(split(rows(z_flux[0])), split(rows(z_faces[0])))
    own_z += products(split(rows(z_flux[1])), split(rows(z_faces[1])))
    for side, other in ((1 - tile_odd, from_z_a), (tile_odd, from_z_b)):
        left = split(rows(z_flux[side, :, side]))
        crosses_z.append(fold(products(left, split(rows(other[0:count]))), count, half))
    for copy in z_stores:
        copy.wait()
    x_stores = [
        pltpu.make_async_copy(x_new.at[0], applied.at[:, 0], sems.at[2]),
        pltpu.make_async_copy(x_new.at[1], applied.at[:, cells_x - 1], sems.at[3]),
    ]
    for copy in x_stores:
        copy.start()
    own_x, crosses_x = 0.0, []
    for flux, mine, other in zip(fluxes_x, (x_a, x_b), (from_x_a, from_x_b)):
        left = split(rows(flux))
        own_x += products(left, split(rows(mine[0:count])))
        crosses_x.append(fold(products(left, split(rows(other[0:count]))), count, cells_z))

    def placing(points, column):
        entry = lax.broadcasted_iota(jnp.int32, (count * points, width), 0)
        at = lax.broadcasted_iota(jnp.int32, (count * points, width), 1)
        return (lax.div(entry, points) + column * count == at).astype(F32)

    scale = 1.0 / (cells_z * length)
    highest = lax.Precision.HIGHEST
    self_rows = own[...] + fold(own_x, count, cells_z)
    stacked = jnp.concatenate([self_rows, -crosses_x[0], -crosses_x[1]], axis=0)
    placed = jnp.dot(stacked, placing(cells_z, tile), precision=highest, preferred_element_type=F32) * scale
    placed_z = jnp.dot(
        jnp.concatenate([fold(own_z, count, cells_x), -crosses_z[0], -crosses_z[1]], axis=1),
        jnp.concatenate(
            [
                placing(cells_x, tile),
                placing(half, tile + 1 - 2 * tile_odd),
                placing(half, tile + 2 * tile_odd - 1),
            ],
            axis=0,
        ),
        precision=highest,
        preferred_element_type=F32,
    )
    blocks[...] = jnp.zeros_like(blocks)
    blocks[slab] = placed[0:count] + placed_z * scale
    blocks[slab + 1 - 2 * slab_odd] = placed[count : 2 * count]
    slot_b = slab + 2 * slab_odd - 1

    @pl.when(jnp.logical_and(slot_b >= 0, slot_b < slots))
    def _():
        blocks[slot_b] = placed[2 * count : 3 * count]

    for copy in x_stores:
        copy.wait()


def finish_kernel(count, tile, coarse):
    size = tile.shape[0]
    row = lax.broadcasted_iota(jnp.int32, (size, size), 0)
    column = lax.broadcasted_iota(jnp.int32, (size, size), 1)
    value = tile[...]
    other = jnp.where(lax.div(row, count) == lax.div(column, count), 0.0, value.T)
    coarse[...] = value + other


def shards(vectors, classes, permittivity):
    count, cells_x, cells_z, length = vectors.shape
    slabs, tiles = lax.axis_size("gx"), lax.axis_size("yz")
    hbm = pl.BlockSpec(memory_space=pltpu.HBM)
    anywhere = pl.BlockSpec(memory_space=pl.ANY)
    vmem = pl.BlockSpec(memory_space=pltpu.VMEM)
    shape = jax.ShapeDtypeStruct
    limit = 24 * 1024 * 1024
    params = pltpu.CompilerParams(vmem_limit_bytes=limit)
    vectors = pltpu.with_memory_space_constraint(vectors, pltpu.HBM)
    classes = pltpu.with_memory_space_constraint(classes, pltpu.HBM)
    permittivity = pltpu.with_memory_space_constraint(permittivity, pltpu.HBM)

    half = cells_x // 2
    own_eps_z = cells_x // half
    x_a, x_b, z_a, z_b = pl.pallas_call(
        faces_kernel,
        out_shape=(
            shape((count + 1, cells_z, length), F32),
            shape((count + 1, cells_z, length), F32),
            shape((count + own_eps_z, half, length), F32),
            shape((count + own_eps_z, half, length), F32),
        ),
        in_specs=[hbm, hbm, hbm],
        out_specs=(vmem,) * 4,
        scratch_shapes=[
            pltpu.VMEM((4, cells_z, length), jnp.int32),
            pltpu.SMEM(permittivity.shape, F32),
            pltpu.SemaphoreType.DMA((9,)),
        ],
        compiler_params=params,
        name="faces",
    )(permittivity, vectors, classes)

    near_x, near_z = [], []
    for slab in range(slabs):
        for tile in range(tiles):
            here = slab * tiles + tile
            mate = (slab + 1 ^ 1) - 1
            near_x.append((here, mate * tiles + tile if 0 <= mate < slabs else slab * tiles + (tile ^ 2)))
            mate = (tile + 1 ^ 1) - 1
            near_z.append((here, slab * tiles + mate if 0 <= mate < tiles else (slab ^ 1) * tiles + tile))
    both = ("gx", "yz")
    from_z_b = lax.ppermute(z_b, both, near_z)
    from_x_b = lax.ppermute(x_b, both, near_x)
    from_z_a = lax.ppermute(z_a, "yz", [(i, i ^ 1) for i in range(tiles)])
    from_x_a = lax.ppermute(x_a, "gx", [(i, i ^ 1) for i in range(slabs)])

    chunks = 4
    applied, own, z_faces, x_sums, z_sums = pl.pallas_call(
        functools.partial(block_kernel, chunks),
        out_shape=(
            pltpu.HBM(vectors.shape, F32),
            shape((count, count * cells_z), F32),
            shape((2, count, cells_x, length), F32),
            shape((2, count, cells_z, length), F32),
            shape((2, count, cells_x, length), F32),
        ),
        in_specs=[hbm, hbm, hbm],
        out_specs=(hbm, vmem, anywhere, anywhere, anywhere),
        scratch_shapes=[
            pltpu.VMEM(vectors.shape, F32),
            pltpu.VMEM(classes.shape, jnp.int32),
            pltpu.VMEM((cells_x + 1, cells_z, length), F32),
            pltpu.VMEM(vectors.shape, F32),
            pltpu.VMEM((2 * count * cells_z, 2 * count * cells_z), F32),
            pltpu.SMEM(permittivity.shape, F32),
            pltpu.SemaphoreType.DMA((8 + 2 * chunks,)),
        ],
        compiler_params=params,
        cost_estimate=pl.CostEstimate(flops=5_000_000_000, bytes_accessed=20_000_000, transcendentals=0),
        name="block",
    )(permittivity, vectors, classes)

    applied, blocks = pl.pallas_call(
        outer_kernel,
        out_shape=(pltpu.HBM(vectors.shape, F32), shape((tiles, count, count * slabs), F32)),
        in_specs=[hbm] + [vmem] * 12,
        out_specs=(hbm, vmem),
        scratch_shapes=[
            pltpu.VMEM((2, count, cells_z, length), F32),
            pltpu.VMEM((2, count, cells_x, length), F32),
            pltpu.VMEM((2, count, 2, half, length), F32),
            pltpu.SemaphoreType.DMA((4,)),
        ],
        input_output_aliases={0: 0},
        compiler_params=params,
        name="outer",
    )(
        applied, own, z_faces, x_sums, z_sums, x_a, x_b, z_a, z_b,
        from_x_a, from_x_b, from_z_a, from_z_b,
    )
    tile = lax.all_to_all(blocks, "yz", split_axis=0, concat_axis=0, tiled=True)
    tile = tile.reshape(tiles * count, count * slabs)
    coarse = pl.pallas_call(
        functools.partial(finish_kernel, count),
        out_shape=shape(tile.shape, F32),
        in_specs=[vmem],
        out_specs=vmem,
        compiler_params=params,
        name="finish",
    )(tile)
    return (applied, coarse)


def solution(mesh):
    return jax.shard_map(
        shards,
        mesh=mesh,
        in_specs=(P(None, "gx", "yz", None), P("gx", "yz", None), P()),
        out_specs=(P(None, "gx", "yz", None), P("gx", "yz")),
        check_vma=False,
    )
```

```python
import functools
import jax
import jax.numpy as jnp
from jax import lax
from jax.experimental import pallas as pl
from jax.experimental.pallas import tpu as pltpu
from jax.sharding import PartitionSpec as P

F32 = jnp.float32
BF16 = jnp.bfloat16


def harmonic(first_value, second_value):
    return 2.0 * first_value * second_value / (first_value + second_value)


def permit(classes, table):
    value = jnp.where(classes == 0, table[0], 0.0)
    for index in range(1, table.shape[0]):
        value = jnp.where(classes == index, table[index], value)
    return value


def split(rows):
    high = rows.astype(BF16)
    low = (rows - high.astype(F32)).astype(BF16)
    return jnp.concatenate([high, low], axis=0)


def products(left, right):
    return lax.dot_general(left, right, (((1,), (1,)), ((), ())), preferred_element_type=F32)


def fold(full, count, points):
    size = count * points
    total = (full[:size, :size] + full[:size, size:]) + (full[size:, :size] + full[size:, size:])
    row = lax.broadcasted_iota(jnp.int32, (size, size), 0)
    column = lax.broadcasted_iota(jnp.int32, (size, size), 1)
    total = jnp.where(row & (points - 1) == column & (points - 1), total, 0.0)
    return jnp.sum(total.reshape(count, points, size), axis=1)


def select(rows, places):
    high = rows.astype(BF16)
    rest = rows - high.astype(F32)
    middle = rest.astype(BF16)
    low = (rest - middle.astype(F32)).astype(BF16)
    parts = jnp.concatenate([high, middle, low], axis=0)
    summed = jnp.dot(parts, places.astype(BF16), preferred_element_type=F32)
    size = rows.shape[0]
    return (summed[2 * size :] + summed[size : 2 * size]) + summed[:size]


def faces_kernel(table_in, vectors, classes, x_a, x_b, z_a, z_b, held, table, sems):
    count, cells_x, cells_z, length = vectors.shape
    half = cells_x // 2
    slab_odd = lax.rem(lax.axis_index("gx"), 2)
    tile_odd = lax.rem(lax.axis_index("yz"), 2)
    table_copy = pltpu.make_async_copy(table_in, table, sems.at[0])
    table_copy.start()
    layers, copies = [], []
    for odd in range(2):
        layer = [
            pltpu.make_async_copy(classes.at[:, (cells_z - 1) * side], held.at[index], sems.at[1 + index])
            for index, side in enumerate((1 - odd, odd))
        ]
        face = [
            pltpu.make_async_copy(
                vectors.at[:, (1 - side) * half : (2 - side) * half, (cells_z - 1) * side],
                out.at[0:count],
                sems.at[5 + index],
            )
            for index, (out, side) in enumerate(((z_a, 1 - odd), (z_b, odd)))
        ]

        @pl.when(tile_odd == odd)
        def _():
            for copy in layer + face:
                copy.start()

        if odd == 0:
            layers += layer
            copies += face
    for index, (out, side) in enumerate(((x_a, 1 - slab_odd), (x_b, slab_odd))):
        at = (cells_x - 1) * side
        layer = pltpu.make_async_copy(classes.at[at], held.at[2 + index], sems.at[3 + index])
        layer.start()
        layers.append(layer)
        face = pltpu.make_async_copy(vectors.at[:, at], out.at[0:count], sems.at[7 + index])
        face.start()
        copies.append(face)
    table_copy.wait()
    for index, out in enumerate((z_a, z_b, x_a, x_b)):
        layers[index].wait()
        out[count:] = permit(held[index], table).reshape(out.shape[0] - count, out.shape[1], length)
    for copy in copies:
        copy.wait()


def block_kernel(
    chunks, table_in, vectors, classes, applied, own, z_faces, x_sums, z_sums,
    held, kinds, face_x, result, total, table, sems,
):
    count, cells_x, cells_z, length = vectors.shape
    step = cells_x // chunks
    kind_copy = pltpu.make_async_copy(classes, kinds, sems.at[0])
    kind_copy.start()
    table_copy = pltpu.make_async_copy(table_in, table, sems.at[7 + 2 * chunks])
    table_copy.start()
    loads, stores = [], []
    for chunk in range(chunks):
        planes = pl.ds(chunk * step, step)
        load = pltpu.make_async_copy(vectors.at[:, planes], held.at[:, planes], sems.at[1 + chunk])
        load.start()
        loads.append(load)
        stores.append(
            pltpu.make_async_copy(result.at[:, planes], applied.at[:, planes], sems.at[1 + chunks + chunk])
        )
    face_x[0] = jnp.zeros((cells_z, length), F32)
    total[...] = jnp.zeros_like(total)
    row = lax.broadcasted_iota(jnp.int32, (cells_z, length), 0)
    column = lax.broadcasted_iota(jnp.int32, (cells_z, length), 1)
    kind_copy.wait()
    table_copy.wait()

    def plane(index):
        before = jnp.maximum(index - 1, 0)
        after = jnp.minimum(index + 1, cells_x - 1)
        value = permit(kinds[index], table)
        value_after = permit(kinds[after], table)
        low_x = face_x[index]
        high_x = jnp.where(index + 1 < cells_x, harmonic(value, value_after), 0.0)
        face_x[index + 1] = high_x
        value_z = pltpu.roll(value, cells_z - 1, 0)
        value_y = pltpu.roll(value, length - 1, 1)
        high_z = jnp.where(row < cells_z - 1, harmonic(value, value_z), 0.0)
        high_y = jnp.where(column < length - 1, harmonic(value, value_y), 0.0)
        for k in range(count):
            here = held[k, index]
            flux = low_x * (here - held[k, before]) + high_x * (here - held[k, after])
            flux_z = high_z * (here - pltpu.roll(here, cells_z - 1, 0))
            flux = flux + (flux_z - pltpu.roll(flux_z, 1, 0))
            flux_y = high_y * (here - pltpu.roll(here, length - 1, 1))
            flux = flux + (flux_y - pltpu.roll(flux_y, 1, 1))
            result[k, index] = flux

    def gram(index):
        left = split(held[:, index].reshape(count * cells_z, length))
        right = split(result[:, index].reshape(count * cells_z, length))
        return products(left, right)

    def follow(index, carry):
        total[...] += gram(index - 1)
        plane(index)
        return carry

    loads[0].wait()
    plane(0)
    for chunk in range(chunks):
        if chunk + 1 < chunks:
            loads[chunk + 1].wait()
        lax.fori_loop(max(1, chunk * step), (chunk + 1) * step, follow, 0)
        stores[chunk].start()
    sides = [
        pltpu.make_async_copy(result.at[:, 0], x_sums.at[0], sems.at[1 + 2 * chunks]),
        pltpu.make_async_copy(result.at[:, cells_x - 1], x_sums.at[1], sems.at[2 + 2 * chunks]),
        pltpu.make_async_copy(result.at[:, :, 0], z_sums.at[0], sems.at[3 + 2 * chunks]),
        pltpu.make_async_copy(result.at[:, :, cells_z - 1], z_sums.at[1], sems.at[4 + 2 * chunks]),
        pltpu.make_async_copy(held.at[:, :, 0], z_faces.at[0], sems.at[5 + 2 * chunks]),
        pltpu.make_async_copy(held.at[:, :, cells_z - 1], z_faces.at[1], sems.at[6 + 2 * chunks]),
    ]
    for copy in sides:
        copy.start()
    own[...] = fold(total[...] + gram(cells_x - 1), count, cells_z)
    for copy in sides + stores:
        copy.wait()


def outer_kernel(
    applied_in, own, z_faces, x_sums, z_sums, x_a, x_b, z_a, z_b, from_x_a, from_x_b, from_z_a, from_z_b,
    applied, x_new, blocks, z_new, z_flux, sems,
):
    count, cells_x, cells_z, length = applied.shape
    slots, _, width = blocks.shape
    half = cells_x // 2
    slab, tile = lax.axis_index("gx"), lax.axis_index("yz")
    slabs, tiles = lax.axis_size("gx"), lax.axis_size("yz")
    slab_odd, tile_odd = lax.rem(slab, 2), lax.rem(tile, 2)

    def rows(block):
        return block.reshape(-1, length)

    crosses_z = []
    for side, mine, other in ((1 - tile_odd, z_a, from_z_a), (tile_odd, z_b, from_z_b)):
        met = jnp.logical_and(tile + 2 * side - 1 >= 0, tile + 2 * side - 1 < tiles)
        weight = jnp.where(met, harmonic(rows(mine[count:]), rows(other[count:])), 0.0)
        flux = z_faces[side] * weight
        z_new[side] = z_sums[side] + flux
        z_flux[side] = flux.reshape(count, 2, half, length)
    stores = [
        pltpu.make_async_copy(z_new.at[0], applied.at[:, :, 0], sems.at[0]),
        pltpu.make_async_copy(z_new.at[1], applied.at[:, :, cells_z - 1], sems.at[1]),
    ]
    for copy in stores:
        copy.start()
    fluxes_x = []
    for side, mine, other in ((1 - slab_odd, x_a, from_x_a), (slab_odd, x_b, from_x_b)):
        met = jnp.logical_and(slab + 2 * side - 1 >= 0, slab + 2 * side - 1 < slabs)
        weight = jnp.where(met, harmonic(mine[count], other[count]), 0.0)
        flux = mine[0:count] * weight
        x_new[side] = x_sums[side] + flux
        fluxes_x.append(flux)
    for side, end in ((0, 0), (1, cells_x - 1)):
        part, at = divmod(end, half)
        x_new[side, :, 0:1, :] += z_flux[0, :, part, at : at + 1, :]
        x_new[side, :, cells_z - 1 : cells_z, :] += z_flux[1, :, part, at : at + 1, :]
    own_z = products(split(rows(z_flux[0])), split(rows(z_faces[0])))
    own_z += products(split(rows(z_flux[1])), split(rows(z_faces[1])))
    for side, other in ((1 - tile_odd, from_z_a), (tile_odd, from_z_b)):
        left = split(rows(z_flux[side, :, side]))
        crosses_z.append(fold(products(left, split(rows(other[0:count]))), count, half))
    own_x, crosses_x = 0.0, []
    for flux, mine, other in zip(fluxes_x, (x_a, x_b), (from_x_a, from_x_b)):
        left = split(rows(flux))
        own_x += products(left, split(rows(mine[0:count])))
        crosses_x.append(fold(products(left, split(rows(other[0:count]))), count, cells_z))

    scale = 1.0 / (cells_z * length)
    entry = lax.broadcasted_iota(jnp.int32, (width, width), 0)
    column = lax.broadcasted_iota(jnp.int32, (width, width), 1)
    place = (entry >> (cells_z.bit_length() - 1)) + tile * count == column
    is_b = entry >= width // 2
    tile_there = jnp.where(is_b, tile + 2 * tile_odd - 1, tile + 1 - 2 * tile_odd)
    place_z = ((entry & (width // 2 - 1)) >> (half.bit_length() - 1)) + tile_there * count == column
    stacked = jnp.concatenate(
        [
            own[...] + fold(own_x, count, cells_z) + fold(own_z, count, cells_x),
            -crosses_x[0],
            -crosses_x[1],
            -jnp.concatenate(crosses_z, axis=1),
        ],
        axis=0,
    )
    placed = select(stacked * scale, jnp.concatenate([place.astype(F32), place_z.astype(F32)], axis=1))
    blocks[...] = jnp.zeros_like(blocks)
    blocks[slab] = placed[0:count, :width] + placed[3 * count :, width:]
    blocks[slab + 1 - 2 * slab_odd] = placed[count : 2 * count, :width]
    slot_b = slab + 2 * slab_odd - 1

    @pl.when(jnp.logical_and(slot_b >= 0, slot_b < slots))
    def _():
        blocks[slot_b] = placed[2 * count : 3 * count, :width]

    for copy in stores:
        copy.wait()


def finish_kernel(count, applied_in, x_new, tile, applied, coarse, summed, sems):
    stores = [
        pltpu.make_async_copy(x_new.at[0], applied.at[:, 0], sems.at[0]),
        pltpu.make_async_copy(x_new.at[1], applied.at[:, applied.shape[1] - 1], sems.at[1]),
    ]
    for copy in stores:
        copy.start()
    size = tile.shape[0]
    row = lax.broadcasted_iota(jnp.int32, (size, size), 0)
    column = lax.broadcasted_iota(jnp.int32, (size, size), 1)
    shift = count.bit_length() - 1
    value = tile[...]
    summed[...] = value + jnp.where(row >> shift == column >> shift, 0.0, value.T)
    stores.append(pltpu.make_async_copy(summed, coarse, sems.at[2]))
    stores[2].start()
    for copy in stores:
        copy.wait()


def shards(vectors, classes, permittivity):
    count, cells_x, cells_z, length = vectors.shape
    slabs, tiles = lax.axis_size("gx"), lax.axis_size("yz")
    hbm = pl.BlockSpec(memory_space=pltpu.HBM)
    anywhere = pl.BlockSpec(memory_space=pl.ANY)
    vmem = pl.BlockSpec(memory_space=pltpu.VMEM)
    shape = jax.ShapeDtypeStruct
    limit = 24 * 1024 * 1024
    params = pltpu.CompilerParams(vmem_limit_bytes=limit)
    vectors = pltpu.with_memory_space_constraint(vectors, pltpu.HBM)
    classes = pltpu.with_memory_space_constraint(classes, pltpu.HBM)
    permittivity = pltpu.with_memory_space_constraint(permittivity, pltpu.HBM)

    half = cells_x // 2
    own_eps_z = cells_x // half
    x_a, x_b, z_a, z_b = pl.pallas_call(
        faces_kernel,
        out_shape=(
            shape((count + 1, cells_z, length), F32),
            shape((count + 1, cells_z, length), F32),
            shape((count + own_eps_z, half, length), F32),
            shape((count + own_eps_z, half, length), F32),
        ),
        in_specs=[hbm, hbm, hbm],
        out_specs=(vmem,) * 4,
        scratch_shapes=[
            pltpu.VMEM((4, cells_z, length), jnp.int32),
            pltpu.SMEM(permittivity.shape, F32),
            pltpu.SemaphoreType.DMA((9,)),
        ],
        compiler_params=params,
        name="faces",
    )(permittivity, vectors, classes)

    near_x, near_z = [], []
    for slab in range(slabs):
        for tile in range(tiles):
            here = slab * tiles + tile
            mate = (slab + 1 ^ 1) - 1
            near_x.append((here, mate * tiles + tile if 0 <= mate < slabs else slab * tiles + (tile ^ 2)))
            mate = (tile + 1 ^ 1) - 1
            near_z.append((here, slab * tiles + mate if 0 <= mate < tiles else (slab ^ 1) * tiles + tile))
    both = ("gx", "yz")
    from_z_b = lax.ppermute(z_b, both, near_z)
    from_x_b = lax.ppermute(x_b, both, near_x)
    from_z_a = lax.ppermute(z_a, "yz", [(i, i ^ 1) for i in range(tiles)])
    from_x_a = lax.ppermute(x_a, "gx", [(i, i ^ 1) for i in range(slabs)])

    chunks = 4
    applied, own, z_faces, x_sums, z_sums = pl.pallas_call(
        functools.partial(block_kernel, chunks),
        out_shape=(
            pltpu.HBM(vectors.shape, F32),
            shape((count, count * cells_z), F32),
            shape((2, count, cells_x, length), F32),
            shape((2, count, cells_z, length), F32),
            shape((2, count, cells_x, length), F32),
        ),
        in_specs=[hbm, hbm, hbm],
        out_specs=(hbm, vmem, anywhere, anywhere, anywhere),
        scratch_shapes=[
            pltpu.VMEM(vectors.shape, F32),
            pltpu.VMEM(classes.shape, jnp.int32),
            pltpu.VMEM((cells_x + 1, cells_z, length), F32),
            pltpu.VMEM(vectors.shape, F32),
            pltpu.VMEM((2 * count * cells_z, 2 * count * cells_z), F32),
            pltpu.SMEM(permittivity.shape, F32),
            pltpu.SemaphoreType.DMA((8 + 2 * chunks,)),
        ],
        compiler_params=params,
        cost_estimate=pl.CostEstimate(flops=5_000_000_000, bytes_accessed=20_000_000, transcendentals=0),
        name="block",
    )(permittivity, vectors, classes)

    applied, x_new, blocks = pl.pallas_call(
        outer_kernel,
        out_shape=(
            pltpu.HBM(vectors.shape, F32),
            shape((2, count, cells_z, length), F32),
            shape((tiles, count, count * slabs), F32),
        ),
        in_specs=[hbm] + [vmem] * 12,
        out_specs=(hbm, vmem, vmem),
        scratch_shapes=[
            pltpu.VMEM((2, count, cells_x, length), F32),
            pltpu.VMEM((2, count, 2, half, length), F32),
            pltpu.SemaphoreType.DMA((2,)),
        ],
        input_output_aliases={0: 0},
        compiler_params=params,
        name="outer",
    )(
        applied, own, z_faces, x_sums, z_sums, x_a, x_b, z_a, z_b,
        from_x_a, from_x_b, from_z_a, from_z_b,
    )
    tile = lax.all_to_all(blocks, "yz", split_axis=0, concat_axis=0, tiled=True)
    tile = tile.reshape(tiles * count, count * slabs)
    return pl.pallas_call(
        functools.partial(finish_kernel, count),
        out_shape=(pltpu.HBM(vectors.shape, F32), pltpu.HBM(tile.shape, F32)),
        in_specs=[hbm, vmem, vmem],
        out_specs=(hbm, hbm),
        scratch_shapes=[pltpu.VMEM(tile.shape, F32), pltpu.SemaphoreType.DMA((3,))],
        input_output_aliases={0: 0},
        compiler_params=params,
        name="finish",
    )(applied, x_new, tile)


def solution(mesh):
    return jax.shard_map(
        shards,
        mesh=mesh,
        in_specs=(P(None, "gx", "yz", None), P("gx", "yz", None), P()),
        out_specs=(P(None, "gx", "yz", None), P("gx", "yz")),
        check_vma=False,
    )
```

```python
import functools
import jax
import jax.numpy as jnp
from jax import lax
from jax.experimental import pallas as pl
from jax.experimental.pallas import tpu as pltpu
from jax.sharding import PartitionSpec as P

F32 = jnp.float32
BF16 = jnp.bfloat16


def harmonic(first_value, second_value):
    return 2.0 * first_value * second_value / (first_value + second_value)


def permit(classes, table):
    value = jnp.where(classes == 0, table[0], 0.0)
    for index in range(1, len(table)):
        value = jnp.where(classes == index, table[index], value)
    return value


def split(rows):
    high = rows.astype(BF16)
    low = (rows - high.astype(F32)).astype(BF16)
    return jnp.concatenate([high, low], axis=0)


def products(left, right):
    return lax.dot_general(left, right, (((1,), (1,)), ((), ())), preferred_element_type=F32)


def fold(full, count, points):
    size = count * points
    total = (full[:size, :size] + full[:size, size:]) + (full[size:, :size] + full[size:, size:])
    row = lax.broadcasted_iota(jnp.int32, (size, size), 0)
    column = lax.broadcasted_iota(jnp.int32, (size, size), 1)
    total = jnp.where(row & (points - 1) == column & (points - 1), total, 0.0)
    return jnp.sum(total.reshape(count, points, size), axis=1)


def select(rows, places):
    high = rows.astype(BF16)
    rest = rows - high.astype(F32)
    middle = rest.astype(BF16)
    low = (rest - middle.astype(F32)).astype(BF16)
    parts = jnp.concatenate([high, middle, low], axis=0)
    summed = jnp.dot(parts, places.astype(BF16), preferred_element_type=F32)
    size = rows.shape[0]
    return (summed[2 * size :] + summed[size : 2 * size]) + summed[:size]


def faces_kernel(table_in, vectors, classes, x_a, x_b, z_a, z_b, levels, held, table_ref, sems):
    count, cells_x, cells_z, length = vectors.shape
    half = cells_x // 2
    slab_odd = lax.rem(lax.axis_index("gx"), 2)
    tile_odd = lax.rem(lax.axis_index("yz"), 2)
    table_copy = pltpu.make_async_copy(table_in, table_ref, sems.at[0])
    table_copy.start()
    layers, copies = [], []
    for odd in range(2):
        layer = [
            pltpu.make_async_copy(classes.at[:, (cells_z - 1) * side], held.at[index], sems.at[1 + index])
            for index, side in enumerate((1 - odd, odd))
        ]
        face = [
            pltpu.make_async_copy(
                vectors.at[:, (1 - side) * half : (2 - side) * half, (cells_z - 1) * side],
                out.at[0:count],
                sems.at[5 + index],
            )
            for index, (out, side) in enumerate(((z_a, 1 - odd), (z_b, odd)))
        ]

        @pl.when(tile_odd == odd)
        def _():
            for copy in layer + face:
                copy.start()

        if odd == 0:
            layers += layer
            copies += face
    for index, (out, side) in enumerate(((x_a, 1 - slab_odd), (x_b, slab_odd))):
        at = (cells_x - 1) * side
        layer = pltpu.make_async_copy(classes.at[at], held.at[2 + index], sems.at[3 + index])
        layer.start()
        layers.append(layer)
        face = pltpu.make_async_copy(vectors.at[:, at], out.at[0:count], sems.at[7 + index])
        face.start()
        copies.append(face)
    table_copy.wait()
    table = [table_ref[index] for index in range(levels.shape[0])]
    row = lax.broadcasted_iota(jnp.int32, levels.shape, 0)
    levels[...] = permit(row, table)
    for index, out in enumerate((z_a, z_b, x_a, x_b)):
        layers[index].wait()
        out[count:] = permit(held[index], table).reshape(out.shape[0] - count, out.shape[1], length)
    for copy in copies:
        copy.wait()


def block_kernel(
    chunks, levels, kinds, vectors, applied, own, z_faces, x_sums, z_sums,
    held, face_x, face_z, face_y, result, total, sems,
):
    count, cells_x, cells_z, length = vectors.shape
    step = cells_x // chunks
    loads, stores = [], []
    for chunk in range(chunks):
        planes = pl.ds(chunk * step, step)
        load = pltpu.make_async_copy(vectors.at[:, planes], held.at[:, planes], sems.at[chunk])
        load.start()
        loads.append(load)
        stores.append(
            pltpu.make_async_copy(result.at[:, planes], applied.at[:, planes], sems.at[chunks + chunk])
        )
    total[...] = jnp.zeros_like(total)
    row = lax.broadcasted_iota(jnp.int32, (cells_z, length), 0)
    column = lax.broadcasted_iota(jnp.int32, (cells_z, length), 1)
    table = [levels[index : index + 1, :] for index in range(levels.shape[0])]
    face_x[0] = jnp.zeros((cells_z, length), F32)

    def weigh(index, value):
        value_after = permit(kinds[jnp.minimum(index + 1, cells_x - 1)], table)
        face_x[index + 1] = jnp.where(index + 1 < cells_x, harmonic(value, value_after), 0.0)
        value_z = pltpu.roll(value, cells_z - 1, 0)
        value_y = pltpu.roll(value, length - 1, 1)
        face_z[index] = jnp.where(row < cells_z - 1, harmonic(value, value_z), 0.0)
        face_y[index] = jnp.where(column < length - 1, harmonic(value, value_y), 0.0)
        return value_after

    lax.fori_loop(0, cells_x, weigh, permit(kinds[0], table))

    def plane(index):
        before = jnp.maximum(index - 1, 0)
        after = jnp.minimum(index + 1, cells_x - 1)
        low_x, high_x = face_x[index], face_x[index + 1]
        high_z, high_y = face_z[index], face_y[index]
        for k in range(count):
            here = held[k, index]
            flux = low_x * (here - held[k, before]) + high_x * (here - held[k, after])
            flux_z = high_z * (here - pltpu.roll(here, cells_z - 1, 0))
            flux = flux + (flux_z - pltpu.roll(flux_z, 1, 0))
            flux_y = high_y * (here - pltpu.roll(here, length - 1, 1))
            flux = flux + (flux_y - pltpu.roll(flux_y, 1, 1))
            result[k, index] = flux

    def gram(index):
        left = split(held[:, index].reshape(count * cells_z, length))
        right = split(result[:, index].reshape(count * cells_z, length))
        return products(left, right)

    def follow(index, carry):
        total[...] += gram(index - 1)
        plane(index)
        return carry

    loads[0].wait()
    plane(0)
    for chunk in range(chunks):
        if chunk + 1 < chunks:
            loads[chunk + 1].wait()
        lax.fori_loop(max(1, chunk * step), (chunk + 1) * step, follow, 0)
        stores[chunk].start()
    sides = [
        pltpu.make_async_copy(result.at[:, 0], x_sums.at[0], sems.at[2 * chunks]),
        pltpu.make_async_copy(result.at[:, cells_x - 1], x_sums.at[1], sems.at[1 + 2 * chunks]),
        pltpu.make_async_copy(result.at[:, :, 0], z_sums.at[0], sems.at[2 + 2 * chunks]),
        pltpu.make_async_copy(result.at[:, :, cells_z - 1], z_sums.at[1], sems.at[3 + 2 * chunks]),
        pltpu.make_async_copy(held.at[:, :, 0], z_faces.at[0], sems.at[4 + 2 * chunks]),
        pltpu.make_async_copy(held.at[:, :, cells_z - 1], z_faces.at[1], sems.at[5 + 2 * chunks]),
    ]
    for copy in sides:
        copy.start()
    own[...] = fold(total[...] + gram(cells_x - 1), count, cells_z)
    for copy in sides + stores:
        copy.wait()


def outer_kernel(
    applied_in, own, z_faces, x_sums, z_sums, x_a, x_b, z_a, z_b, from_x_a, from_x_b, from_z_a, from_z_b,
    applied, x_new, blocks, z_new, z_flux, sems,
):
    count, cells_x, cells_z, length = applied.shape
    slots, _, width = blocks.shape
    half = cells_x // 2
    slab, tile = lax.axis_index("gx"), lax.axis_index("yz")
    slabs, tiles = lax.axis_size("gx"), lax.axis_size("yz")
    slab_odd, tile_odd = lax.rem(slab, 2), lax.rem(tile, 2)

    def rows(block):
        return block.reshape(-1, length)

    crosses_z = []
    for side, mine, other in ((1 - tile_odd, z_a, from_z_a), (tile_odd, z_b, from_z_b)):
        met = jnp.logical_and(tile + 2 * side - 1 >= 0, tile + 2 * side - 1 < tiles)
        weight = jnp.where(met, harmonic(rows(mine[count:]), rows(other[count:])), 0.0)
        flux = z_faces[side] * weight
        z_new[side] = z_sums[side] + flux
        z_flux[side] = flux.reshape(count, 2, half, length)
    stores = [
        pltpu.make_async_copy(z_new.at[0], applied.at[:, :, 0], sems.at[0]),
        pltpu.make_async_copy(z_new.at[1], applied.at[:, :, cells_z - 1], sems.at[1]),
    ]
    for copy in stores:
        copy.start()
    fluxes_x = []
    for side, mine, other in ((1 - slab_odd, x_a, from_x_a), (slab_odd, x_b, from_x_b)):
        met = jnp.logical_and(slab + 2 * side - 1 >= 0, slab + 2 * side - 1 < slabs)
        weight = jnp.where(met, harmonic(mine[count], other[count]), 0.0)
        flux = mine[0:count] * weight
        x_new[side] = x_sums[side] + flux
        fluxes_x.append(flux)
    for side, end in ((0, 0), (1, cells_x - 1)):
        part, at = divmod(end, half)
        x_new[side, :, 0:1, :] += z_flux[0, :, part, at : at + 1, :]
        x_new[side, :, cells_z - 1 : cells_z, :] += z_flux[1, :, part, at : at + 1, :]
    own_z = products(split(rows(z_flux[0])), split(rows(z_faces[0])))
    own_z += products(split(rows(z_flux[1])), split(rows(z_faces[1])))
    for side, other in ((1 - tile_odd, from_z_a), (tile_odd, from_z_b)):
        left = split(rows(z_flux[side, :, side]))
        crosses_z.append(fold(products(left, split(rows(other[0:count]))), count, half))
    own_x, crosses_x = 0.0, []
    for flux, mine, other in zip(fluxes_x, (x_a, x_b), (from_x_a, from_x_b)):
        left = split(rows(flux))
        own_x += products(left, split(rows(mine[0:count])))
        crosses_x.append(fold(products(left, split(rows(other[0:count]))), count, cells_z))

    scale = 1.0 / (cells_z * length)
    entry = lax.broadcasted_iota(jnp.int32, (width, width), 0)
    column = lax.broadcasted_iota(jnp.int32, (width, width), 1)
    place = (entry >> (cells_z.bit_length() - 1)) + tile * count == column
    is_b = entry >= width // 2
    tile_there = jnp.where(is_b, tile + 2 * tile_odd - 1, tile + 1 - 2 * tile_odd)
    place_z = ((entry & (width // 2 - 1)) >> (half.bit_length() - 1)) + tile_there * count == column
    stacked = jnp.concatenate(
        [
            own[...] + fold(own_x, count, cells_z) + fold(own_z, count, cells_x),
            -crosses_x[0],
            -crosses_x[1],
            -jnp.concatenate(crosses_z, axis=1),
        ],
        axis=0,
    )
    placed = select(stacked * scale, jnp.concatenate([place.astype(F32), place_z.astype(F32)], axis=1))
    blocks[...] = jnp.zeros_like(blocks)
    blocks[slab] = placed[0:count, :width] + placed[3 * count :, width:]
    blocks[slab + 1 - 2 * slab_odd] = placed[count : 2 * count, :width]
    slot_b = slab + 2 * slab_odd - 1

    @pl.when(jnp.logical_and(slot_b >= 0, slot_b < slots))
    def _():
        blocks[slot_b] = placed[2 * count : 3 * count, :width]

    for copy in stores:
        copy.wait()


def finish_kernel(count, applied_in, x_new, tile, applied, coarse, summed, sems):
    stores = [
        pltpu.make_async_copy(x_new.at[0], applied.at[:, 0], sems.at[0]),
        pltpu.make_async_copy(x_new.at[1], applied.at[:, applied.shape[1] - 1], sems.at[1]),
    ]
    for copy in stores:
        copy.start()
    size = tile.shape[0]
    row = lax.broadcasted_iota(jnp.int32, (size, size), 0)
    column = lax.broadcasted_iota(jnp.int32, (size, size), 1)
    shift = count.bit_length() - 1
    value = tile[...]
    summed[...] = value + jnp.where(row >> shift == column >> shift, 0.0, value.T)
    stores.append(pltpu.make_async_copy(summed, coarse, sems.at[2]))
    stores[2].start()
    for copy in stores:
        copy.wait()


def shards(vectors, classes, permittivity):
    count, cells_x, cells_z, length = vectors.shape
    slabs, tiles = lax.axis_size("gx"), lax.axis_size("yz")
    hbm = pl.BlockSpec(memory_space=pltpu.HBM)
    anywhere = pl.BlockSpec(memory_space=pl.ANY)
    vmem = pl.BlockSpec(memory_space=pltpu.VMEM)
    shape = jax.ShapeDtypeStruct
    limit = 24 * 1024 * 1024
    params = pltpu.CompilerParams(vmem_limit_bytes=limit)
    classes_in = classes
    vectors = pltpu.with_memory_space_constraint(vectors, pltpu.HBM)
    classes = pltpu.with_memory_space_constraint(classes, pltpu.HBM)
    permittivity = pltpu.with_memory_space_constraint(permittivity, pltpu.HBM)

    half = cells_x // 2
    own_eps_z = cells_x // half
    x_a, x_b, z_a, z_b, levels = pl.pallas_call(
        faces_kernel,
        out_shape=(
            shape((count + 1, cells_z, length), F32),
            shape((count + 1, cells_z, length), F32),
            shape((count + own_eps_z, half, length), F32),
            shape((count + own_eps_z, half, length), F32),
            shape((permittivity.shape[0], length), F32),
        ),
        in_specs=[hbm, hbm, hbm],
        out_specs=(vmem,) * 5,
        scratch_shapes=[
            pltpu.VMEM((4, cells_z, length), jnp.int32),
            pltpu.SMEM(permittivity.shape, F32),
            pltpu.SemaphoreType.DMA((9,)),
        ],
        compiler_params=params,
        name="faces",
    )(permittivity, vectors, classes)

    near_x, near_z = [], []
    for slab in range(slabs):
        for tile in range(tiles):
            here = slab * tiles + tile
            mate = (slab + 1 ^ 1) - 1
            near_x.append((here, mate * tiles + tile if 0 <= mate < slabs else slab * tiles + (tile ^ 2)))
            mate = (tile + 1 ^ 1) - 1
            near_z.append((here, slab * tiles + mate if 0 <= mate < tiles else (slab ^ 1) * tiles + tile))
    both = ("gx", "yz")
    from_z_b = lax.ppermute(z_b, both, near_z)
    from_x_b = lax.ppermute(x_b, both, near_x)
    from_z_a = lax.ppermute(z_a, "yz", [(i, i ^ 1) for i in range(tiles)])
    from_x_a = lax.ppermute(x_a, "gx", [(i, i ^ 1) for i in range(slabs)])

    chunks = 4
    applied, own, z_faces, x_sums, z_sums = pl.pallas_call(
        functools.partial(block_kernel, chunks),
        out_shape=(
            pltpu.HBM(vectors.shape, F32),
            shape((count, count * cells_z), F32),
            shape((2, count, cells_x, length), F32),
            shape((2, count, cells_z, length), F32),
            shape((2, count, cells_x, length), F32),
        ),
        in_specs=[vmem, vmem, hbm],
        out_specs=(hbm, vmem, anywhere, anywhere, anywhere),
        scratch_shapes=[
            pltpu.VMEM(vectors.shape, F32),
            pltpu.VMEM((cells_x + 1, cells_z, length), F32),
            pltpu.VMEM(classes.shape, F32),
            pltpu.VMEM(classes.shape, F32),
            pltpu.VMEM(vectors.shape, F32),
            pltpu.VMEM((2 * count * cells_z, 2 * count * cells_z), F32),
            pltpu.SemaphoreType.DMA((6 + 2 * chunks,)),
        ],
        compiler_params=params,
        cost_estimate=pl.CostEstimate(flops=5_000_000_000, bytes_accessed=20_000_000, transcendentals=0),
        name="block",
    )(levels, classes_in, vectors)

    applied, x_new, blocks = pl.pallas_call(
        outer_kernel,
        out_shape=(
            pltpu.HBM(vectors.shape, F32),
            shape((2, count, cells_z, length), F32),
            shape((tiles, count, count * slabs), F32),
        ),
        in_specs=[hbm] + [vmem] * 12,
        out_specs=(hbm, vmem, vmem),
        scratch_shapes=[
            pltpu.VMEM((2, count, cells_x, length), F32),
            pltpu.VMEM((2, count, 2, half, length), F32),
            pltpu.SemaphoreType.DMA((2,)),
        ],
        input_output_aliases={0: 0},
        compiler_params=params,
        name="outer",
    )(
        applied, own, z_faces, x_sums, z_sums, x_a, x_b, z_a, z_b,
        from_x_a, from_x_b, from_z_a, from_z_b,
    )
    tile = lax.all_to_all(blocks, "yz", split_axis=0, concat_axis=0, tiled=True)
    tile = tile.reshape(tiles * count, count * slabs)
    return pl.pallas_call(
        functools.partial(finish_kernel, count),
        out_shape=(pltpu.HBM(vectors.shape, F32), pltpu.HBM(tile.shape, F32)),
        in_specs=[hbm, vmem, vmem],
        out_specs=(hbm, hbm),
        scratch_shapes=[pltpu.VMEM(tile.shape, F32), pltpu.SemaphoreType.DMA((3,))],
        input_output_aliases={0: 0},
        compiler_params=params,
        name="finish",
    )(applied, x_new, tile)


def solution(mesh):
    return jax.shard_map(
        shards,
        mesh=mesh,
        in_specs=(P(None, "gx", "yz", None), P("gx", "yz", None), P()),
        out_specs=(P(None, "gx", "yz", None), P("gx", "yz")),
        check_vma=False,
    )
```

```python
import functools
import jax
import jax.numpy as jnp
from jax import lax
from jax.experimental import pallas as pl
from jax.experimental.pallas import tpu as pltpu
from jax.sharding import PartitionSpec as P

F32 = jnp.float32
BF16 = jnp.bfloat16


def harmonic(first_value, second_value):
    return 2.0 * first_value * second_value / (first_value + second_value)


def permit(classes, table):
    value = jnp.where(classes == 0, table[0], 0.0)
    for index in range(1, len(table)):
        value = jnp.where(classes == index, table[index], value)
    return value


def split(rows):
    high = rows.astype(BF16)
    low = (rows - high.astype(F32)).astype(BF16)
    return jnp.concatenate([high, low], axis=0)


def products(left, right):
    return lax.dot_general(left, right, (((1,), (1,)), ((), ())), preferred_element_type=F32)


def fold(full, count, points):
    size = count * points
    total = (full[:size, :size] + full[:size, size:]) + (full[size:, :size] + full[size:, size:])
    row = lax.broadcasted_iota(jnp.int32, (size, size), 0)
    column = lax.broadcasted_iota(jnp.int32, (size, size), 1)
    total = jnp.where(row & (points - 1) == column & (points - 1), total, 0.0)
    return jnp.sum(total.reshape(count, points, size), axis=1)


def select(rows, places):
    high = rows.astype(BF16)
    rest = rows - high.astype(F32)
    middle = rest.astype(BF16)
    low = (rest - middle.astype(F32)).astype(BF16)
    parts = jnp.concatenate([high, middle, low], axis=0)
    summed = jnp.dot(parts, places.astype(BF16), preferred_element_type=F32)
    size = rows.shape[0]
    return (summed[2 * size :] + summed[size : 2 * size]) + summed[:size]


def faces_kernel(table_in, vectors, classes, x_a, x_b, z_a, z_b, levels, held, table_ref, sems):
    count, cells_x, cells_z, length = vectors.shape
    half = cells_x // 2
    slab_odd = lax.rem(lax.axis_index("gx"), 2)
    tile_odd = lax.rem(lax.axis_index("yz"), 2)
    table_copy = pltpu.make_async_copy(table_in, table_ref, sems.at[0])
    table_copy.start()
    layers, copies = [], []
    for odd in range(2):
        layer = [
            pltpu.make_async_copy(classes.at[:, (cells_z - 1) * side], held.at[index], sems.at[1 + index])
            for index, side in enumerate((1 - odd, odd))
        ]
        face = [
            pltpu.make_async_copy(
                vectors.at[:, (1 - side) * half : (2 - side) * half, (cells_z - 1) * side],
                out.at[0:count],
                sems.at[5 + index],
            )
            for index, (out, side) in enumerate(((z_a, 1 - odd), (z_b, odd)))
        ]

        @pl.when(tile_odd == odd)
        def _():
            for copy in layer + face:
                copy.start()

        if odd == 0:
            layers += layer
            copies += face
    for index, (out, side) in enumerate(((x_a, 1 - slab_odd), (x_b, slab_odd))):
        at = (cells_x - 1) * side
        layer = pltpu.make_async_copy(classes.at[at], held.at[2 + index], sems.at[3 + index])
        layer.start()
        layers.append(layer)
        face = pltpu.make_async_copy(vectors.at[:, at], out.at[0:count], sems.at[7 + index])
        face.start()
        copies.append(face)
    table_copy.wait()
    table = [table_ref[index] for index in range(levels.shape[0])]
    row = lax.broadcasted_iota(jnp.int32, levels.shape, 0)
    levels[...] = permit(row, table)
    for index, out in enumerate((z_a, z_b, x_a, x_b)):
        layers[index].wait()
        out[count:] = permit(held[index], table).reshape(out.shape[0] - count, out.shape[1], length)
    for copy in copies:
        copy.wait()


def block_kernel(
    chunks, levels, kinds, vectors, applied, own, z_faces, x_sums, z_sums,
    held, face_x, face_z, face_y, result, total, sems,
):
    count, cells_x, cells_z, length = vectors.shape
    step = cells_x // chunks
    loads, stores = [], []
    for chunk in range(chunks):
        planes = pl.ds(chunk * step, step)
        load = pltpu.make_async_copy(vectors.at[:, planes], held.at[:, planes], sems.at[chunk])
        load.start()
        loads.append(load)
        stores.append(
            pltpu.make_async_copy(result.at[:, planes], applied.at[:, planes], sems.at[chunks + chunk])
        )
    total[...] = jnp.zeros_like(total)
    row = lax.broadcasted_iota(jnp.int32, (cells_z, length), 0)
    column = lax.broadcasted_iota(jnp.int32, (cells_z, length), 1)
    table = [levels[index : index + 1, :] for index in range(levels.shape[0])]
    face_x[0] = jnp.zeros((cells_z, length), F32)

    def weigh(index, value):
        value_after = permit(kinds[jnp.minimum(index + 1, cells_x - 1)], table)
        face_x[index + 1] = jnp.where(index + 1 < cells_x, harmonic(value, value_after), 0.0)
        value_z = pltpu.roll(value, cells_z - 1, 0)
        value_y = pltpu.roll(value, length - 1, 1)
        face_z[index] = jnp.where(row < cells_z - 1, harmonic(value, value_z), 0.0)
        face_y[index] = jnp.where(column < length - 1, harmonic(value, value_y), 0.0)
        return value_after

    lax.fori_loop(0, cells_x, weigh, permit(kinds[0], table))

    def plane(index):
        before = jnp.maximum(index - 1, 0)
        after = jnp.minimum(index + 1, cells_x - 1)
        low_x, high_x = face_x[index], face_x[index + 1]
        high_z, high_y = face_z[index], face_y[index]
        for k in range(count):
            here = held[k, index]
            flux = low_x * (here - held[k, before]) + high_x * (here - held[k, after])
            flux_z = high_z * (here - pltpu.roll(here, cells_z - 1, 0))
            flux = flux + (flux_z - pltpu.roll(flux_z, 1, 0))
            flux_y = high_y * (here - pltpu.roll(here, length - 1, 1))
            flux = flux + (flux_y - pltpu.roll(flux_y, 1, 1))
            result[k, index] = flux

    def gram(index):
        left = split(held[:, index].reshape(count * cells_z, length))
        right = split(result[:, index].reshape(count * cells_z, length))
        return products(left, right)

    def follow(index, carry):
        total[...] += gram(index - 1)
        plane(index)
        return carry

    loads[0].wait()
    plane(0)
    for chunk in range(chunks):
        if chunk + 1 < chunks:
            loads[chunk + 1].wait()
        lax.fori_loop(max(1, chunk * step), (chunk + 1) * step, follow, 0)
        stores[chunk].start()
    sides = [
        pltpu.make_async_copy(result.at[:, 0], x_sums.at[0], sems.at[2 * chunks]),
        pltpu.make_async_copy(result.at[:, cells_x - 1], x_sums.at[1], sems.at[1 + 2 * chunks]),
        pltpu.make_async_copy(result.at[:, :, 0], z_sums.at[0], sems.at[2 + 2 * chunks]),
        pltpu.make_async_copy(result.at[:, :, cells_z - 1], z_sums.at[1], sems.at[3 + 2 * chunks]),
        pltpu.make_async_copy(held.at[:, :, 0], z_faces.at[0], sems.at[4 + 2 * chunks]),
        pltpu.make_async_copy(held.at[:, :, cells_z - 1], z_faces.at[1], sems.at[5 + 2 * chunks]),
    ]
    for copy in sides:
        copy.start()
    own[...] = fold(total[...] + gram(cells_x - 1), count, cells_z)
    for copy in sides + stores:
        copy.wait()


def outer_kernel(
    applied_in, own, z_faces, x_sums, z_sums, z_a, z_b, x_b, x_a, from_x_a, from_x_b, from_z_a, from_z_b,
    applied, x_new, blocks, z_new, z_flux, sems,
):
    count, cells_x, cells_z, length = applied.shape
    slots, _, width = blocks.shape
    half = cells_x // 2
    slab, tile = lax.axis_index("gx"), lax.axis_index("yz")
    slabs, tiles = lax.axis_size("gx"), lax.axis_size("yz")
    slab_odd, tile_odd = lax.rem(slab, 2), lax.rem(tile, 2)

    def rows(block):
        return block.reshape(-1, length)

    crosses_z = []
    for side, mine, other in ((1 - tile_odd, z_a, from_z_a), (tile_odd, z_b, from_z_b)):
        met = jnp.logical_and(tile + 2 * side - 1 >= 0, tile + 2 * side - 1 < tiles)
        weight = jnp.where(met, harmonic(rows(mine[count:]), rows(other[count:])), 0.0)
        flux = z_faces[side] * weight
        z_new[side] = z_sums[side] + flux
        z_flux[side] = flux.reshape(count, 2, half, length)
    stores = [
        pltpu.make_async_copy(z_new.at[0], applied.at[:, :, 0], sems.at[0]),
        pltpu.make_async_copy(z_new.at[1], applied.at[:, :, cells_z - 1], sems.at[1]),
    ]
    for copy in stores:
        copy.start()
    fluxes_x = []
    for side, mine, other in ((1 - slab_odd, x_a, from_x_a), (slab_odd, x_b, from_x_b)):
        met = jnp.logical_and(slab + 2 * side - 1 >= 0, slab + 2 * side - 1 < slabs)
        weight = jnp.where(met, harmonic(mine[count], other[count]), 0.0)
        flux = mine[0:count] * weight
        x_new[side] = x_sums[side] + flux
        fluxes_x.append(flux)
    for side, end in ((0, 0), (1, cells_x - 1)):
        part, at = divmod(end, half)
        x_new[side, :, 0:1, :] += z_flux[0, :, part, at : at + 1, :]
        x_new[side, :, cells_z - 1 : cells_z, :] += z_flux[1, :, part, at : at + 1, :]
    own_z = products(split(rows(z_flux[0])), split(rows(z_faces[0])))
    own_z += products(split(rows(z_flux[1])), split(rows(z_faces[1])))
    for side, other in ((1 - tile_odd, from_z_a), (tile_odd, from_z_b)):
        left = split(rows(z_flux[side, :, side]))
        crosses_z.append(fold(products(left, split(rows(other[0:count]))), count, half))
    own_x, crosses_x = 0.0, []
    for flux, mine, other in zip(fluxes_x, (x_a, x_b), (from_x_a, from_x_b)):
        left = split(rows(flux))
        own_x += products(left, split(rows(mine[0:count])))
        crosses_x.append(fold(products(left, split(rows(other[0:count]))), count, cells_z))

    scale = 1.0 / (cells_z * length)
    entry = lax.broadcasted_iota(jnp.int32, (width, width), 0)
    column = lax.broadcasted_iota(jnp.int32, (width, width), 1)
    place = (entry >> (cells_z.bit_length() - 1)) + tile * count == column
    is_b = entry >= width // 2
    tile_there = jnp.where(is_b, tile + 2 * tile_odd - 1, tile + 1 - 2 * tile_odd)
    place_z = ((entry & (width // 2 - 1)) >> (half.bit_length() - 1)) + tile_there * count == column
    stacked = jnp.concatenate(
        [
            own[...] + fold(own_x, count, cells_z) + fold(own_z, count, cells_x),
            -crosses_x[0],
            -crosses_x[1],
            -jnp.concatenate(crosses_z, axis=1),
        ],
        axis=0,
    )
    placed = select(stacked * scale, jnp.concatenate([place.astype(F32), place_z.astype(F32)], axis=1))
    blocks[...] = jnp.zeros_like(blocks)
    blocks[slab] = placed[0:count, :width] + placed[3 * count :, width:]
    blocks[slab + 1 - 2 * slab_odd] = placed[count : 2 * count, :width]
    slot_b = slab + 2 * slab_odd - 1

    @pl.when(jnp.logical_and(slot_b >= 0, slot_b < slots))
    def _():
        blocks[slot_b] = placed[2 * count : 3 * count, :width]

    for copy in stores:
        copy.wait()


def finish_kernel(count, applied_in, x_new, tile, applied, coarse, summed, sems):
    stores = [
        pltpu.make_async_copy(x_new.at[0], applied.at[:, 0], sems.at[0]),
        pltpu.make_async_copy(x_new.at[1], applied.at[:, applied.shape[1] - 1], sems.at[1]),
    ]
    for copy in stores:
        copy.start()
    size = tile.shape[0]
    row = lax.broadcasted_iota(jnp.int32, (size, size), 0)
    column = lax.broadcasted_iota(jnp.int32, (size, size), 1)
    shift = count.bit_length() - 1
    value = tile[...]
    summed[...] = value + jnp.where(row >> shift == column >> shift, 0.0, value.T)
    stores.append(pltpu.make_async_copy(summed, coarse, sems.at[2]))
    stores[2].start()
    for copy in stores:
        copy.wait()


def shards(vectors, classes, permittivity):
    count, cells_x, cells_z, length = vectors.shape
    slabs, tiles = lax.axis_size("gx"), lax.axis_size("yz")
    hbm = pl.BlockSpec(memory_space=pltpu.HBM)
    anywhere = pl.BlockSpec(memory_space=pl.ANY)
    vmem = pl.BlockSpec(memory_space=pltpu.VMEM)
    shape = jax.ShapeDtypeStruct
    limit = 24 * 1024 * 1024
    params = pltpu.CompilerParams(vmem_limit_bytes=limit)
    classes_in = classes
    vectors = pltpu.with_memory_space_constraint(vectors, pltpu.HBM)
    classes = pltpu.with_memory_space_constraint(classes, pltpu.HBM)
    permittivity = pltpu.with_memory_space_constraint(permittivity, pltpu.HBM)

    half = cells_x // 2
    own_eps_z = cells_x // half
    x_a, x_b, z_a, z_b, levels = pl.pallas_call(
        faces_kernel,
        out_shape=(
            shape((count + 1, cells_z, length), F32),
            shape((count + 1, cells_z, length), F32),
            shape((count + own_eps_z, half, length), F32),
            shape((count + own_eps_z, half, length), F32),
            shape((permittivity.shape[0], length), F32),
        ),
        in_specs=[hbm, hbm, hbm],
        out_specs=(vmem,) * 5,
        scratch_shapes=[
            pltpu.VMEM((4, cells_z, length), jnp.int32),
            pltpu.SMEM(permittivity.shape, F32),
            pltpu.SemaphoreType.DMA((9,)),
        ],
        compiler_params=params,
        name="faces",
    )(permittivity, vectors, classes)

    near_x, near_z = [], []
    for slab in range(slabs):
        for tile in range(tiles):
            here = slab * tiles + tile
            mate = (slab + 1 ^ 1) - 1
            near_x.append((here, mate * tiles + tile if 0 <= mate < slabs else slab * tiles + (tile ^ 2)))
            mate = (tile + 1 ^ 1) - 1
            near_z.append((here, slab * tiles + mate if 0 <= mate < tiles else (slab ^ 1) * tiles + tile))
    both = ("gx", "yz")
    from_z_b = lax.ppermute(z_b, both, near_z)
    from_x_b = lax.ppermute(x_b, both, near_x)
    from_z_a = lax.ppermute(z_a, "yz", [(i, i ^ 1) for i in range(tiles)])
    from_x_a = lax.ppermute(x_a, "gx", [(i, i ^ 1) for i in range(slabs)])

    chunks = 4
    applied, own, z_faces, x_sums, z_sums = pl.pallas_call(
        functools.partial(block_kernel, chunks),
        out_shape=(
            pltpu.HBM(vectors.shape, F32),
            shape((count, count * cells_z), F32),
            shape((2, count, cells_x, length), F32),
            shape((2, count, cells_z, length), F32),
            shape((2, count, cells_x, length), F32),
        ),
        in_specs=[vmem, vmem, hbm],
        out_specs=(hbm, vmem, anywhere, anywhere, anywhere),
        scratch_shapes=[
            pltpu.VMEM(vectors.shape, F32),
            pltpu.VMEM((cells_x + 1, cells_z, length), F32),
            pltpu.VMEM(classes.shape, F32),
            pltpu.VMEM(classes.shape, F32),
            pltpu.VMEM(vectors.shape, F32),
            pltpu.VMEM((2 * count * cells_z, 2 * count * cells_z), F32),
            pltpu.SemaphoreType.DMA((6 + 2 * chunks,)),
        ],
        compiler_params=params,
        cost_estimate=pl.CostEstimate(flops=5_000_000_000, bytes_accessed=20_000_000, transcendentals=0),
        name="block",
    )(levels, classes_in, vectors)

    applied, x_new, blocks = pl.pallas_call(
        outer_kernel,
        out_shape=(
            pltpu.HBM(vectors.shape, F32),
            shape((2, count, cells_z, length), F32),
            shape((tiles, count, count * slabs), F32),
        ),
        in_specs=[hbm] + [vmem] * 12,
        out_specs=(hbm, vmem, vmem),
        scratch_shapes=[
            pltpu.VMEM((2, count, cells_x, length), F32),
            pltpu.VMEM((2, count, 2, half, length), F32),
            pltpu.SemaphoreType.DMA((2,)),
        ],
        input_output_aliases={0: 0},
        compiler_params=params,
        name="outer",
    )(
        applied, own, z_faces, x_sums, z_sums, z_a, z_b, x_b, x_a,
        from_x_a, from_x_b, from_z_a, from_z_b,
    )
    tile = lax.all_to_all(blocks, "yz", split_axis=0, concat_axis=0, tiled=True)
    tile = tile.reshape(tiles * count, count * slabs)
    return pl.pallas_call(
        functools.partial(finish_kernel, count),
        out_shape=(pltpu.HBM(vectors.shape, F32), pltpu.HBM(tile.shape, F32)),
        in_specs=[hbm, vmem, vmem],
        out_specs=(hbm, hbm),
        scratch_shapes=[pltpu.VMEM(tile.shape, F32), pltpu.SemaphoreType.DMA((3,))],
        input_output_aliases={0: 0},
        compiler_params=params,
        name="finish",
    )(applied, x_new, tile)


def solution(mesh):
    return jax.shard_map(
        shards,
        mesh=mesh,
        in_specs=(P(None, "gx", "yz", None), P("gx", "yz", None), P()),
        out_specs=(P(None, "gx", "yz", None), P("gx", "yz")),
        check_vma=False,
    )
```

```python
import functools
import jax
import jax.numpy as jnp
from jax import lax
from jax.experimental import pallas as pl
from jax.experimental.pallas import tpu as pltpu
from jax.sharding import PartitionSpec as P

F32 = jnp.float32
BF16 = jnp.bfloat16


def harmonic(first_value, second_value):
    return 2.0 * first_value * second_value / (first_value + second_value)


def permit(classes, table):
    value = jnp.where(classes == 0, table[0], 0.0)
    for index in range(1, len(table)):
        value = jnp.where(classes == index, table[index], value)
    return value


def split(rows):
    high = rows.astype(BF16)
    low = (rows - high.astype(F32)).astype(BF16)
    return jnp.concatenate([high, low], axis=0)


def products(left, right):
    return lax.dot_general(left, right, (((1,), (1,)), ((), ())), preferred_element_type=F32)


def fold(full, count, points):
    size = count * points
    total = (full[:size, :size] + full[:size, size:]) + (full[size:, :size] + full[size:, size:])
    row = lax.broadcasted_iota(jnp.int32, (size, size), 0)
    column = lax.broadcasted_iota(jnp.int32, (size, size), 1)
    total = jnp.where(row & (points - 1) == column & (points - 1), total, 0.0)
    return jnp.sum(total.reshape(count, points, size), axis=1)


def select(rows, places):
    high = rows.astype(BF16)
    rest = rows - high.astype(F32)
    middle = rest.astype(BF16)
    low = (rest - middle.astype(F32)).astype(BF16)
    parts = jnp.concatenate([high, middle, low], axis=0)
    summed = jnp.dot(parts, places.astype(BF16), preferred_element_type=F32)
    size = rows.shape[0]
    return (summed[2 * size :] + summed[size : 2 * size]) + summed[:size]


def faces_kernel(table_in, vectors, classes, x_a, x_b, z_a, z_b, levels, held, table_ref, sems):
    count, cells_x, cells_z, length = vectors.shape
    half = cells_x // 2
    slab_odd = lax.rem(lax.axis_index("gx"), 2)
    tile_odd = lax.rem(lax.axis_index("yz"), 2)
    table_copy = pltpu.make_async_copy(table_in, table_ref, sems.at[0])
    table_copy.start()
    layers, copies = [], []
    for odd in range(2):
        layer = [
            pltpu.make_async_copy(classes.at[:, (cells_z - 1) * side], held.at[index], sems.at[1 + index])
            for index, side in enumerate((1 - odd, odd))
        ]
        face = [
            pltpu.make_async_copy(
                vectors.at[:, (1 - side) * half : (2 - side) * half, (cells_z - 1) * side],
                out.at[0:count],
                sems.at[5 + index],
            )
            for index, (out, side) in enumerate(((z_a, 1 - odd), (z_b, odd)))
        ]

        @pl.when(tile_odd == odd)
        def _():
            for copy in layer + face:
                copy.start()

        if odd == 0:
            layers += layer
            copies += face
    for index, (out, side) in enumerate(((x_a, 1 - slab_odd), (x_b, slab_odd))):
        at = (cells_x - 1) * side
        layer = pltpu.make_async_copy(classes.at[at], held.at[2 + index], sems.at[3 + index])
        layer.start()
        layers.append(layer)
        face = pltpu.make_async_copy(vectors.at[:, at], out.at[0:count], sems.at[7 + index])
        face.start()
        copies.append(face)
    table_copy.wait()
    table = [table_ref[index] for index in range(levels.shape[0])]
    row = lax.broadcasted_iota(jnp.int32, levels.shape, 0)
    levels[...] = permit(row, table)
    for index, out in enumerate((z_a, z_b, x_a, x_b)):
        layers[index].wait()
        out[count:] = permit(held[index], table).reshape(out.shape[0] - count, out.shape[1], length)
    for copy in copies:
        copy.wait()


def block_kernel(
    chunks, levels, kinds, vectors, applied, own, z_faces, x_sums, z_sums,
    held, face_x, face_z, face_y, result, total, sems,
):
    count, cells_x, cells_z, length = vectors.shape
    step = cells_x // chunks
    loads, stores = [], []
    for chunk in range(chunks):
        planes = pl.ds(chunk * step, step)
        load = pltpu.make_async_copy(vectors.at[:, planes], held.at[:, planes], sems.at[chunk])
        load.start()
        loads.append(load)
        stores.append(
            pltpu.make_async_copy(result.at[:, planes], applied.at[:, planes], sems.at[chunks + chunk])
        )
    total[...] = jnp.zeros_like(total)
    row = lax.broadcasted_iota(jnp.int32, (cells_z, length), 0)
    column = lax.broadcasted_iota(jnp.int32, (cells_z, length), 1)
    table = [levels[index : index + 1, :] for index in range(levels.shape[0])]
    face_x[0] = jnp.zeros((cells_z, length), F32)

    def weigh(index, value):
        value_after = permit(kinds[jnp.minimum(index + 1, cells_x - 1)], table)
        face_x[index + 1] = jnp.where(index + 1 < cells_x, harmonic(value, value_after), 0.0)
        value_z = pltpu.roll(value, cells_z - 1, 0)
        value_y = pltpu.roll(value, length - 1, 1)
        face_z[index] = jnp.where(row < cells_z - 1, harmonic(value, value_z), 0.0)
        face_y[index] = jnp.where(column < length - 1, harmonic(value, value_y), 0.0)
        return value_after

    lax.fori_loop(0, cells_x, weigh, permit(kinds[0], table))

    def plane(index):
        before = jnp.maximum(index - 1, 0)
        after = jnp.minimum(index + 1, cells_x - 1)
        low_x, high_x = face_x[index], face_x[index + 1]
        high_z, high_y = face_z[index], face_y[index]
        for k in range(count):
            here = held[k, index]
            flux = low_x * (here - held[k, before]) + high_x * (here - held[k, after])
            flux_z = high_z * (here - pltpu.roll(here, cells_z - 1, 0))
            flux = flux + (flux_z - pltpu.roll(flux_z, 1, 0))
            flux_y = high_y * (here - pltpu.roll(here, length - 1, 1))
            flux = flux + (flux_y - pltpu.roll(flux_y, 1, 1))
            result[k, index] = flux

    def gram(index):
        left = split(held[:, index].reshape(count * cells_z, length))
        right = split(result[:, index].reshape(count * cells_z, length))
        return products(left, right)

    def follow(index, carry):
        total[...] += gram(index - 1)
        plane(index)
        return carry

    loads[0].wait()
    plane(0)
    for chunk in range(chunks):
        if chunk + 1 < chunks:
            loads[chunk + 1].wait()
        lax.fori_loop(max(1, chunk * step), (chunk + 1) * step, follow, 0)
        stores[chunk].start()
    sides = [
        pltpu.make_async_copy(result.at[:, 0], x_sums.at[0], sems.at[2 * chunks]),
        pltpu.make_async_copy(result.at[:, cells_x - 1], x_sums.at[1], sems.at[1 + 2 * chunks]),
        pltpu.make_async_copy(result.at[:, :, 0], z_sums.at[0], sems.at[2 + 2 * chunks]),
        pltpu.make_async_copy(result.at[:, :, cells_z - 1], z_sums.at[1], sems.at[3 + 2 * chunks]),
        pltpu.make_async_copy(held.at[:, :, 0], z_faces.at[0], sems.at[4 + 2 * chunks]),
        pltpu.make_async_copy(held.at[:, :, cells_z - 1], z_faces.at[1], sems.at[5 + 2 * chunks]),
    ]
    for copy in sides:
        copy.start()
    own[...] = fold(total[...] + gram(cells_x - 1), count, cells_z)
    for copy in sides + stores:
        copy.wait()


def outer_kernel(
    applied_in, own, z_faces, x_sums, z_sums, z_a, z_b, x_b, x_a, from_x_a, from_x_b, from_z_a, from_z_b,
    applied, x_new, blocks, z_new, z_flux, sems,
):
    count, cells_x, cells_z, length = applied.shape
    slots, _, width = blocks.shape
    half = cells_x // 2
    slab, tile = lax.axis_index("gx"), lax.axis_index("yz")
    slabs, tiles = lax.axis_size("gx"), lax.axis_size("yz")
    slab_odd, tile_odd = lax.rem(slab, 2), lax.rem(tile, 2)

    def rows(block):
        return block.reshape(-1, length)

    crosses_z = []
    for side, mine, other in ((1 - tile_odd, z_a, from_z_a), (tile_odd, z_b, from_z_b)):
        met = jnp.logical_and(tile + 2 * side - 1 >= 0, tile + 2 * side - 1 < tiles)
        weight = jnp.where(met, harmonic(rows(mine[count:]), rows(other[count:])), 0.0)
        flux = z_faces[side] * weight
        z_new[side] = z_sums[side] + flux
        z_flux[side] = flux.reshape(count, 2, half, length)
    stores = [
        pltpu.make_async_copy(z_new.at[0], applied.at[:, :, 0], sems.at[0]),
        pltpu.make_async_copy(z_new.at[1], applied.at[:, :, cells_z - 1], sems.at[1]),
    ]
    for copy in stores:
        copy.start()
    fluxes_x = []
    for side, mine, other in ((1 - slab_odd, x_a, from_x_a), (slab_odd, x_b, from_x_b)):
        met = jnp.logical_and(slab + 2 * side - 1 >= 0, slab + 2 * side - 1 < slabs)
        weight = jnp.where(met, harmonic(mine[count], other[count]), 0.0)
        flux = mine[0:count] * weight
        x_new[side] = x_sums[side] + flux
        fluxes_x.append(flux)
    for side, end in ((0, 0), (1, cells_x - 1)):
        part, at = divmod(end, half)
        x_new[side, :, 0:1, :] += z_flux[0, :, part, at : at + 1, :]
        x_new[side, :, cells_z - 1 : cells_z, :] += z_flux[1, :, part, at : at + 1, :]
    lefts = [split(rows(z_flux[0])), split(rows(z_flux[1]))]
    rights = [split(rows(z_faces[0])), split(rows(z_faces[1]))]
    for side, other in ((1 - tile_odd, from_z_a), (tile_odd, from_z_b)):
        left = split(rows(z_flux[side, :, side]))
        crosses_z.append(fold(products(left, split(rows(other[0:count]))), count, half))
    crosses_x = []
    for flux, mine, other in zip(fluxes_x, (x_a, x_b), (from_x_a, from_x_b)):
        left = split(rows(flux))
        lefts.append(left)
        rights.append(split(rows(mine[0:count])))
        crosses_x.append(fold(products(left, split(rows(other[0:count]))), count, cells_z))

    own_outer = products(jnp.concatenate(lefts, axis=1), jnp.concatenate(rights, axis=1))
    scale = 1.0 / (cells_z * length)
    entry = lax.broadcasted_iota(jnp.int32, (width, width), 0)
    column = lax.broadcasted_iota(jnp.int32, (width, width), 1)
    place = (entry >> (cells_z.bit_length() - 1)) + tile * count == column
    is_b = entry >= width // 2
    tile_there = jnp.where(is_b, tile + 2 * tile_odd - 1, tile + 1 - 2 * tile_odd)
    place_z = ((entry & (width // 2 - 1)) >> (half.bit_length() - 1)) + tile_there * count == column
    stacked = jnp.concatenate(
        [
            own[...] + fold(own_outer, count, cells_z),
            -crosses_x[0],
            -crosses_x[1],
            -jnp.concatenate(crosses_z, axis=1),
        ],
        axis=0,
    )
    placed = select(stacked * scale, jnp.concatenate([place.astype(F32), place_z.astype(F32)], axis=1))
    blocks[...] = jnp.zeros_like(blocks)
    blocks[slab] = placed[0:count, :width] + placed[3 * count :, width:]
    blocks[slab + 1 - 2 * slab_odd] = placed[count : 2 * count, :width]
    slot_b = slab + 2 * slab_odd - 1

    @pl.when(jnp.logical_and(slot_b >= 0, slot_b < slots))
    def _():
        blocks[slot_b] = placed[2 * count : 3 * count, :width]

    for copy in stores:
        copy.wait()


def finish_kernel(count, applied_in, x_new, tile, applied, coarse, summed, sems):
    stores = [
        pltpu.make_async_copy(x_new.at[0], applied.at[:, 0], sems.at[0]),
        pltpu.make_async_copy(x_new.at[1], applied.at[:, applied.shape[1] - 1], sems.at[1]),
    ]
    for copy in stores:
        copy.start()
    size = tile.shape[0]
    row = lax.broadcasted_iota(jnp.int32, (size, size), 0)
    column = lax.broadcasted_iota(jnp.int32, (size, size), 1)
    shift = count.bit_length() - 1
    value = tile[...]
    summed[...] = value + jnp.where(row >> shift == column >> shift, 0.0, value.T)
    stores.append(pltpu.make_async_copy(summed, coarse, sems.at[2]))
    stores[2].start()
    for copy in stores:
        copy.wait()


def shards(vectors, classes, permittivity):
    count, cells_x, cells_z, length = vectors.shape
    slabs, tiles = lax.axis_size("gx"), lax.axis_size("yz")
    hbm = pl.BlockSpec(memory_space=pltpu.HBM)
    anywhere = pl.BlockSpec(memory_space=pl.ANY)
    vmem = pl.BlockSpec(memory_space=pltpu.VMEM)
    shape = jax.ShapeDtypeStruct
    limit = 24 * 1024 * 1024
    params = pltpu.CompilerParams(vmem_limit_bytes=limit)
    classes_in = classes
    vectors = pltpu.with_memory_space_constraint(vectors, pltpu.HBM)
    classes = pltpu.with_memory_space_constraint(classes, pltpu.HBM)
    permittivity = pltpu.with_memory_space_constraint(permittivity, pltpu.HBM)

    half = cells_x // 2
    own_eps_z = cells_x // half
    x_a, x_b, z_a, z_b, levels = pl.pallas_call(
        faces_kernel,
        out_shape=(
            shape((count + 1, cells_z, length), F32),
            shape((count + 1, cells_z, length), F32),
            shape((count + own_eps_z, half, length), F32),
            shape((count + own_eps_z, half, length), F32),
            shape((permittivity.shape[0], length), F32),
        ),
        in_specs=[hbm, hbm, hbm],
        out_specs=(vmem,) * 5,
        scratch_shapes=[
            pltpu.VMEM((4, cells_z, length), jnp.int32),
            pltpu.SMEM(permittivity.shape, F32),
            pltpu.SemaphoreType.DMA((9,)),
        ],
        compiler_params=params,
        name="faces",
    )(permittivity, vectors, classes)

    near_x, near_z = [], []
    for slab in range(slabs):
        for tile in range(tiles):
            here = slab * tiles + tile
            mate = (slab + 1 ^ 1) - 1
            near_x.append((here, mate * tiles + tile if 0 <= mate < slabs else slab * tiles + (tile ^ 2)))
            mate = (tile + 1 ^ 1) - 1
            near_z.append((here, slab * tiles + mate if 0 <= mate < tiles else (slab ^ 1) * tiles + tile))
    both = ("gx", "yz")
    from_z_b = lax.ppermute(z_b, both, near_z)
    from_x_b = lax.ppermute(x_b, both, near_x)
    from_z_a = lax.ppermute(z_a, "yz", [(i, i ^ 1) for i in range(tiles)])
    from_x_a = lax.ppermute(x_a, "gx", [(i, i ^ 1) for i in range(slabs)])

    chunks = 4
    applied, own, z_faces, x_sums, z_sums = pl.pallas_call(
        functools.partial(block_kernel, chunks),
        out_shape=(
            pltpu.HBM(vectors.shape, F32),
            shape((count, count * cells_z), F32),
            shape((2, count, cells_x, length), F32),
            shape((2, count, cells_z, length), F32),
            shape((2, count, cells_x, length), F32),
        ),
        in_specs=[vmem, vmem, hbm],
        out_specs=(hbm, vmem, anywhere, anywhere, anywhere),
        scratch_shapes=[
            pltpu.VMEM(vectors.shape, F32),
            pltpu.VMEM((cells_x + 1, cells_z, length), F32),
            pltpu.VMEM(classes.shape, F32),
            pltpu.VMEM(classes.shape, F32),
            pltpu.VMEM(vectors.shape, F32),
            pltpu.VMEM((2 * count * cells_z, 2 * count * cells_z), F32),
            pltpu.SemaphoreType.DMA((6 + 2 * chunks,)),
        ],
        compiler_params=params,
        cost_estimate=pl.CostEstimate(flops=5_000_000_000, bytes_accessed=20_000_000, transcendentals=0),
        name="block",
    )(levels, classes_in, vectors)

    applied, x_new, blocks = pl.pallas_call(
        outer_kernel,
        out_shape=(
            pltpu.HBM(vectors.shape, F32),
            shape((2, count, cells_z, length), F32),
            shape((tiles, count, count * slabs), F32),
        ),
        in_specs=[hbm] + [vmem] * 12,
        out_specs=(hbm, vmem, vmem),
        scratch_shapes=[
            pltpu.VMEM((2, count, cells_x, length), F32),
            pltpu.VMEM((2, count, 2, half, length), F32),
            pltpu.SemaphoreType.DMA((2,)),
        ],
        input_output_aliases={0: 0},
        compiler_params=params,
        name="outer",
    )(
        applied, own, z_faces, x_sums, z_sums, z_a, z_b, x_b, x_a,
        from_x_a, from_x_b, from_z_a, from_z_b,
    )
    tile = lax.all_to_all(blocks, "yz", split_axis=0, concat_axis=0, tiled=True)
    tile = tile.reshape(tiles * count, count * slabs)
    return pl.pallas_call(
        functools.partial(finish_kernel, count),
        out_shape=(pltpu.HBM(vectors.shape, F32), pltpu.HBM(tile.shape, F32)),
        in_specs=[hbm, vmem, vmem],
        out_specs=(hbm, hbm),
        scratch_shapes=[pltpu.VMEM(tile.shape, F32), pltpu.SemaphoreType.DMA((3,))],
        input_output_aliases={0: 0},
        compiler_params=params,
        name="finish",
    )(applied, x_new, tile)


def solution(mesh):
    return jax.shard_map(
        shards,
        mesh=mesh,
        in_specs=(P(None, "gx", "yz", None), P("gx", "yz", None), P()),
        out_specs=(P(None, "gx", "yz", None), P("gx", "yz")),
        check_vma=False,
    )
```

```python
import functools
import jax
import jax.numpy as jnp
from jax import lax
from jax.experimental import pallas as pl
from jax.experimental.pallas import tpu as pltpu
from jax.sharding import PartitionSpec as P

F32 = jnp.float32
BF16 = jnp.bfloat16


def harmonic(first_value, second_value):
    return 2.0 * first_value * second_value / (first_value + second_value)


def permit(classes, table):
    value = jnp.where(classes == 0, table[0], 0.0)
    for index in range(1, len(table)):
        value = jnp.where(classes == index, table[index], value)
    return value


def split(rows):
    high = rows.astype(BF16)
    low = (rows - high.astype(F32)).astype(BF16)
    return jnp.concatenate([high, low], axis=0)


def products(left, right):
    return lax.dot_general(left, right, (((1,), (1,)), ((), ())), preferred_element_type=F32)


def fold(full, count, points):
    size = count * points
    total = (full[:size, :size] + full[:size, size:]) + (full[size:, :size] + full[size:, size:])
    row = lax.broadcasted_iota(jnp.int32, (size, size), 0)
    column = lax.broadcasted_iota(jnp.int32, (size, size), 1)
    total = jnp.where(row & (points - 1) == column & (points - 1), total, 0.0)
    return jnp.sum(total.reshape(count, points, size), axis=1)


def select(rows, places):
    high = rows.astype(BF16)
    rest = rows - high.astype(F32)
    middle = rest.astype(BF16)
    low = (rest - middle.astype(F32)).astype(BF16)
    parts = jnp.concatenate([high, middle, low], axis=0)
    summed = jnp.dot(parts, places.astype(BF16), preferred_element_type=F32)
    size = rows.shape[0]
    return (summed[2 * size :] + summed[size : 2 * size]) + summed[:size]


def faces_kernel(table_in, vectors, classes, x_a, x_b, z_a, z_b, levels, held, table_ref, sems):
    count, cells_x, cells_z, length = vectors.shape
    half = cells_x // 2
    slab_odd = lax.rem(lax.axis_index("gx"), 2)
    tile_odd = lax.rem(lax.axis_index("yz"), 2)
    table_copy = pltpu.make_async_copy(table_in, table_ref, sems.at[0])
    table_copy.start()
    layers, copies = [], []
    for odd in range(2):
        layer = [
            pltpu.make_async_copy(classes.at[:, (cells_z - 1) * side], held.at[index], sems.at[1 + index])
            for index, side in enumerate((1 - odd, odd))
        ]
        face = [
            pltpu.make_async_copy(
                vectors.at[:, (1 - side) * half : (2 - side) * half, (cells_z - 1) * side],
                out.at[0:count],
                sems.at[5 + index],
            )
            for index, (out, side) in enumerate(((z_a, 1 - odd), (z_b, odd)))
        ]

        @pl.when(tile_odd == odd)
        def _():
            for copy in layer + face:
                copy.start()

        if odd == 0:
            layers += layer
            copies += face
    for index, (out, side) in enumerate(((x_a, 1 - slab_odd), (x_b, slab_odd))):
        at = (cells_x - 1) * side
        layer = pltpu.make_async_copy(classes.at[at], held.at[2 + index], sems.at[3 + index])
        layer.start()
        layers.append(layer)
        face = pltpu.make_async_copy(vectors.at[:, at], out.at[0:count], sems.at[7 + index])
        face.start()
        copies.append(face)
    table_copy.wait()
    table = [table_ref[index] for index in range(levels.shape[0])]
    row = lax.broadcasted_iota(jnp.int32, levels.shape, 0)
    levels[...] = permit(row, table)
    for index, out in enumerate((z_a, z_b, x_a, x_b)):
        layers[index].wait()
        out[count:] = permit(held[index], table).reshape(out.shape[0] - count, out.shape[1], length)
    for copy in copies:
        copy.wait()


def block_kernel(
    chunks, levels, kinds, vectors, applied, own, z_faces, x_sums, z_sums,
    held, face_x, face_z, face_y, result, total, sems,
):
    count, cells_x, cells_z, length = vectors.shape
    step = cells_x // chunks
    loads, stores = [], []
    for chunk in range(chunks):
        planes = pl.ds(chunk * step, step)
        load = pltpu.make_async_copy(vectors.at[:, planes], held.at[:, planes], sems.at[chunk])
        load.start()
        loads.append(load)
        stores.append(
            pltpu.make_async_copy(result.at[:, planes], applied.at[:, planes], sems.at[chunks + chunk])
        )
    total[...] = jnp.zeros_like(total)
    row = lax.broadcasted_iota(jnp.int32, (cells_z, length), 0)
    column = lax.broadcasted_iota(jnp.int32, (cells_z, length), 1)
    table = [levels[index : index + 1, :] for index in range(levels.shape[0])]
    face_x[0] = jnp.zeros((cells_z, length), F32)

    def weigh(index, value):
        value_after = permit(kinds[jnp.minimum(index + 1, cells_x - 1)], table)
        face_x[index + 1] = jnp.where(index + 1 < cells_x, harmonic(value, value_after), 0.0)
        value_z = pltpu.roll(value, cells_z - 1, 0)
        value_y = pltpu.roll(value, length - 1, 1)
        face_z[index] = jnp.where(row < cells_z - 1, harmonic(value, value_z), 0.0)
        face_y[index] = jnp.where(column < length - 1, harmonic(value, value_y), 0.0)
        return value_after

    lax.fori_loop(0, cells_x, weigh, permit(kinds[0], table))

    def plane(index):
        before = jnp.maximum(index - 1, 0)
        after = jnp.minimum(index + 1, cells_x - 1)
        low_x, high_x = face_x[index], face_x[index + 1]
        high_z, high_y = face_z[index], face_y[index]
        for k in range(count):
            here = held[k, index]
            flux = low_x * (here - held[k, before]) + high_x * (here - held[k, after])
            flux_z = high_z * (here - pltpu.roll(here, cells_z - 1, 0))
            flux = flux + (flux_z - pltpu.roll(flux_z, 1, 0))
            flux_y = high_y * (here - pltpu.roll(here, length - 1, 1))
            flux = flux + (flux_y - pltpu.roll(flux_y, 1, 1))
            result[k, index] = flux

    def gram(index):
        left = split(held[:, index].reshape(count * cells_z, length))
        right = split(result[:, index].reshape(count * cells_z, length))
        return products(left, right)

    def follow(index, carry):
        total[...] += gram(index - 1)
        plane(index)
        return carry

    near = pltpu.make_async_copy(result.at[:, 0], x_sums.at[0], sems.at[2 * chunks])
    loads[0].wait()
    plane(0)
    for chunk in range(chunks):
        if chunk + 1 < chunks:
            loads[chunk + 1].wait()
        lax.fori_loop(max(1, chunk * step), (chunk + 1) * step, follow, 0)
        stores[chunk].start()
        if chunk == 0:
            near.start()
    sides = [
        pltpu.make_async_copy(result.at[:, cells_x - 1], x_sums.at[1], sems.at[1 + 2 * chunks]),
        pltpu.make_async_copy(result.at[:, :, 0], z_sums.at[0], sems.at[2 + 2 * chunks]),
        pltpu.make_async_copy(result.at[:, :, cells_z - 1], z_sums.at[1], sems.at[3 + 2 * chunks]),
        pltpu.make_async_copy(held.at[:, :, 0], z_faces.at[0], sems.at[4 + 2 * chunks]),
        pltpu.make_async_copy(held.at[:, :, cells_z - 1], z_faces.at[1], sems.at[5 + 2 * chunks]),
    ]
    for copy in sides:
        copy.start()
    own[...] = fold(total[...] + gram(cells_x - 1), count, cells_z)
    for copy in [near] + sides + stores:
        copy.wait()


def outer_kernel(
    applied_in, own, z_faces, x_sums, z_sums, z_a, z_b, x_b, x_a, from_x_a, from_x_b, from_z_a, from_z_b,
    applied, x_new, blocks, z_new, z_flux, sems,
):
    count, cells_x, cells_z, length = applied.shape
    slots, _, width = blocks.shape
    half = cells_x // 2
    slab, tile = lax.axis_index("gx"), lax.axis_index("yz")
    slabs, tiles = lax.axis_size("gx"), lax.axis_size("yz")
    slab_odd, tile_odd = lax.rem(slab, 2), lax.rem(tile, 2)

    def rows(block):
        return block.reshape(-1, length)

    crosses_z = []
    for side, mine, other in ((1 - tile_odd, z_a, from_z_a), (tile_odd, z_b, from_z_b)):
        met = jnp.logical_and(tile + 2 * side - 1 >= 0, tile + 2 * side - 1 < tiles)
        weight = jnp.where(met, harmonic(rows(mine[count:]), rows(other[count:])), 0.0)
        flux = z_faces[side] * weight
        z_new[side] = z_sums[side] + flux
        z_flux[side] = flux.reshape(count, 2, half, length)
    stores = [
        pltpu.make_async_copy(z_new.at[0], applied.at[:, :, 0], sems.at[0]),
        pltpu.make_async_copy(z_new.at[1], applied.at[:, :, cells_z - 1], sems.at[1]),
    ]
    for copy in stores:
        copy.start()
    fluxes_x = []
    for side, mine, other in ((1 - slab_odd, x_a, from_x_a), (slab_odd, x_b, from_x_b)):
        met = jnp.logical_and(slab + 2 * side - 1 >= 0, slab + 2 * side - 1 < slabs)
        weight = jnp.where(met, harmonic(mine[count], other[count]), 0.0)
        flux = mine[0:count] * weight
        x_new[side] = x_sums[side] + flux
        fluxes_x.append(flux)
    for side, end in ((0, 0), (1, cells_x - 1)):
        part, at = divmod(end, half)
        x_new[side, :, 0:1, :] += z_flux[0, :, part, at : at + 1, :]
        x_new[side, :, cells_z - 1 : cells_z, :] += z_flux[1, :, part, at : at + 1, :]
    lefts = [split(rows(z_flux[0])), split(rows(z_flux[1]))]
    rights = [split(rows(z_faces[0])), split(rows(z_faces[1]))]
    for side, other in ((1 - tile_odd, from_z_a), (tile_odd, from_z_b)):
        left = split(rows(z_flux[side, :, side]))
        crosses_z.append(fold(products(left, split(rows(other[0:count]))), count, half))
    crosses_x = []
    for flux, mine, other in zip(fluxes_x, (x_a, x_b), (from_x_a, from_x_b)):
        left = split(rows(flux))
        lefts.append(left)
        rights.append(split(rows(mine[0:count])))
        crosses_x.append(fold(products(left, split(rows(other[0:count]))), count, cells_z))

    own_outer = products(jnp.concatenate(lefts, axis=1), jnp.concatenate(rights, axis=1))
    scale = 1.0 / (cells_z * length)
    entry = lax.broadcasted_iota(jnp.int32, (width, width), 0)
    column = lax.broadcasted_iota(jnp.int32, (width, width), 1)
    place = (entry >> (cells_z.bit_length() - 1)) + tile * count == column
    is_b = entry >= width // 2
    tile_there = jnp.where(is_b, tile + 2 * tile_odd - 1, tile + 1 - 2 * tile_odd)
    place_z = ((entry & (width // 2 - 1)) >> (half.bit_length() - 1)) + tile_there * count == column
    stacked = jnp.concatenate(
        [
            own[...] + fold(own_outer, count, cells_z),
            -crosses_x[0],
            -crosses_x[1],
            -jnp.concatenate(crosses_z, axis=1),
        ],
        axis=0,
    )
    placed = select(stacked * scale, jnp.concatenate([place.astype(F32), place_z.astype(F32)], axis=1))
    blocks[...] = jnp.zeros_like(blocks)
    blocks[slab] = placed[0:count, :width] + placed[3 * count :, width:]
    blocks[slab + 1 - 2 * slab_odd] = placed[count : 2 * count, :width]
    slot_b = slab + 2 * slab_odd - 1

    @pl.when(jnp.logical_and(slot_b >= 0, slot_b < slots))
    def _():
        blocks[slot_b] = placed[2 * count : 3 * count, :width]

    for copy in stores:
        copy.wait()


def finish_kernel(count, applied_in, x_new, tile, applied, coarse, summed, sems):
    stores = [
        pltpu.make_async_copy(x_new.at[0], applied.at[:, 0], sems.at[0]),
        pltpu.make_async_copy(x_new.at[1], applied.at[:, applied.shape[1] - 1], sems.at[1]),
    ]
    for copy in stores:
        copy.start()
    size = tile.shape[0]
    row = lax.broadcasted_iota(jnp.int32, (size, size), 0)
    column = lax.broadcasted_iota(jnp.int32, (size, size), 1)
    shift = count.bit_length() - 1
    value = tile[...]
    summed[...] = value + jnp.where(row >> shift == column >> shift, 0.0, value.T)
    stores.append(pltpu.make_async_copy(summed, coarse, sems.at[2]))
    stores[2].start()
    for copy in stores:
        copy.wait()


def shards(vectors, classes, permittivity):
    count, cells_x, cells_z, length = vectors.shape
    slabs, tiles = lax.axis_size("gx"), lax.axis_size("yz")
    hbm = pl.BlockSpec(memory_space=pltpu.HBM)
    anywhere = pl.BlockSpec(memory_space=pl.ANY)
    vmem = pl.BlockSpec(memory_space=pltpu.VMEM)
    shape = jax.ShapeDtypeStruct
    limit = 24 * 1024 * 1024
    params = pltpu.CompilerParams(vmem_limit_bytes=limit)
    classes_in = classes
    vectors = pltpu.with_memory_space_constraint(vectors, pltpu.HBM)
    classes = pltpu.with_memory_space_constraint(classes, pltpu.HBM)
    permittivity = pltpu.with_memory_space_constraint(permittivity, pltpu.HBM)

    half = cells_x // 2
    own_eps_z = cells_x // half
    x_a, x_b, z_a, z_b, levels = pl.pallas_call(
        faces_kernel,
        out_shape=(
            shape((count + 1, cells_z, length), F32),
            shape((count + 1, cells_z, length), F32),
            shape((count + own_eps_z, half, length), F32),
            shape((count + own_eps_z, half, length), F32),
            shape((permittivity.shape[0], length), F32),
        ),
        in_specs=[hbm, hbm, hbm],
        out_specs=(vmem,) * 5,
        scratch_shapes=[
            pltpu.VMEM((4, cells_z, length), jnp.int32),
            pltpu.SMEM(permittivity.shape, F32),
            pltpu.SemaphoreType.DMA((9,)),
        ],
        compiler_params=params,
        name="faces",
    )(permittivity, vectors, classes)

    near_x, near_z = [], []
    for slab in range(slabs):
        for tile in range(tiles):
            here = slab * tiles + tile
            mate = (slab + 1 ^ 1) - 1
            near_x.append((here, mate * tiles + tile if 0 <= mate < slabs else slab * tiles + (tile ^ 2)))
            mate = (tile + 1 ^ 1) - 1
            near_z.append((here, slab * tiles + mate if 0 <= mate < tiles else (slab ^ 1) * tiles + tile))
    both = ("gx", "yz")
    from_z_b = lax.ppermute(z_b, both, near_z)
    from_x_b = lax.ppermute(x_b, both, near_x)
    from_z_a = lax.ppermute(z_a, "yz", [(i, i ^ 1) for i in range(tiles)])
    from_x_a = lax.ppermute(x_a, "gx", [(i, i ^ 1) for i in range(slabs)])

    chunks = 4
    applied, own, z_faces, x_sums, z_sums = pl.pallas_call(
        functools.partial(block_kernel, chunks),
        out_shape=(
            pltpu.HBM(vectors.shape, F32),
            shape((count, count * cells_z), F32),
            shape((2, count, cells_x, length), F32),
            shape((2, count, cells_z, length), F32),
            shape((2, count, cells_x, length), F32),
        ),
        in_specs=[vmem, vmem, hbm],
        out_specs=(hbm, vmem, anywhere, anywhere, anywhere),
        scratch_shapes=[
            pltpu.VMEM(vectors.shape, F32),
            pltpu.VMEM((cells_x + 1, cells_z, length), F32),
            pltpu.VMEM(classes.shape, F32),
            pltpu.VMEM(classes.shape, F32),
            pltpu.VMEM(vectors.shape, F32),
            pltpu.VMEM((2 * count * cells_z, 2 * count * cells_z), F32),
            pltpu.SemaphoreType.DMA((6 + 2 * chunks,)),
        ],
        compiler_params=params,
        cost_estimate=pl.CostEstimate(flops=5_000_000_000, bytes_accessed=20_000_000, transcendentals=0),
        name="block",
    )(levels, classes_in, vectors)

    applied, x_new, blocks = pl.pallas_call(
        outer_kernel,
        out_shape=(
            pltpu.HBM(vectors.shape, F32),
            shape((2, count, cells_z, length), F32),
            shape((tiles, count, count * slabs), F32),
        ),
        in_specs=[hbm] + [vmem] * 12,
        out_specs=(hbm, vmem, vmem),
        scratch_shapes=[
            pltpu.VMEM((2, count, cells_x, length), F32),
            pltpu.VMEM((2, count, 2, half, length), F32),
            pltpu.SemaphoreType.DMA((2,)),
        ],
        input_output_aliases={0: 0},
        compiler_params=params,
        name="outer",
    )(
        applied, own, z_faces, x_sums, z_sums, z_a, z_b, x_b, x_a,
        from_x_a, from_x_b, from_z_a, from_z_b,
    )
    tile = lax.all_to_all(blocks, "yz", split_axis=0, concat_axis=0, tiled=True)
    tile = tile.reshape(tiles * count, count * slabs)
    return pl.pallas_call(
        functools.partial(finish_kernel, count),
        out_shape=(pltpu.HBM(vectors.shape, F32), pltpu.HBM(tile.shape, F32)),
        in_specs=[hbm, vmem, vmem],
        out_specs=(hbm, hbm),
        scratch_shapes=[pltpu.VMEM(tile.shape, F32), pltpu.SemaphoreType.DMA((3,))],
        input_output_aliases={0: 0},
        compiler_params=params,
        name="finish",
    )(applied, x_new, tile)


def solution(mesh):
    return jax.shard_map(
        shards,
        mesh=mesh,
        in_specs=(P(None, "gx", "yz", None), P("gx", "yz", None), P()),
        out_specs=(P(None, "gx", "yz", None), P("gx", "yz")),
        check_vma=False,
    )
```
